256 devices in a mesh: band: 64 (over y, z_hi, x), batch: 4 (over z_lo, core).
Axes of the slice: x: 4, y: 4, z: 8 (z_hi: 4, z_lo: 2; z = z_hi * 2 + z_lo), core: 2. Of those that a mesh axis runs over, the one named last changes fastest.
Arguments:
- activations: bfloat16 [4, 64, 256, 768], P('batch', 'band'), may hold values from -36 to 36, as said below
- cotangent: bfloat16 [4, 64, 256, 768], P('batch', 'band'), may hold values from -6 to 6
- qkv_weight: bfloat16 [768, 2304], replicated, as said below
- out_weight: bfloat16 [768, 768], replicated, may hold values from -0.21875 to 0.21875
Outputs:
- grads_in: bfloat16 [4, 64, 256, 768], P('batch', 'band')
- qkv_grad: float32 [768, 2304], P('band')
- out_grad: float32 [768, 768], P('band')
The draws below stay inside these ranges and needn't reach their ends.
Inputs may be any that keep to these rules, and one draw needn't show every extreme that they name: `activations`: each token's features are random values times a scale of the token and a scale of the feature, both between 0.3 and 3. `qkv_weight`: entries lie within 29 / sqrt(768) in magnitude.
All inputs are finite; a program needn't handle non-finite values.
Results may differ from the reference program's by a relative error of at most 0.014.
Values may be sent and summed in bfloat16 or wider, within the bound.
A program may use at most 64 MiB of HBM per device.

```python
import math
import jax
import jax.numpy as jnp
from jax import lax

D = 768
HEADS = 12
HD = 64
WID = 256
HGT = 64
SAMPLES = 4


def draw_activations(key, part):
    key = jax.random.fold_in(key, 11)
    streams = jax.random.split(key, 3)
    shape = (SAMPLES, HGT, WID, D)
    row_scale = jnp.exp(jax.random.uniform(streams[0], (SAMPLES, HGT, WID, 1), jnp.float32, math.log(0.3), math.log(3.0)))
    chan_scale = jnp.exp(jax.random.uniform(streams[1], (D,), jnp.float32, math.log(0.3), math.log(3.0)))
    base = jnp.clip(jax.random.normal(streams[2], shape, jnp.float32), -4.0, 4.0)
    return (base * row_scale * chan_scale).astype(jnp.bfloat16)


def draw_qkv_weight(key, part):
    key = jax.random.fold_in(key, 23)
    streams = jax.random.split(key, 1)
    whole = jnp.clip(jax.random.normal(streams[0], (D, 3, HEADS, HD), jnp.float32), -4.0, 4.0)
    return (whole.reshape(D, 3 * D) * D ** (-0.5)).astype(jnp.bfloat16)


def block_levels(rng, extent, shards, smallest, top_value):
    gain = 1.0
    for dim, parts in shards:
        steps = jax.random.uniform(jax.random.fold_in(jax.random.fold_in(rng, 6), dim), (parts,), jnp.float32, smallest / len(shards), top_value / len(shards))
        gain = gain * jnp.repeat(jnp.exp(steps), extent[dim] // parts).reshape((-1,) + (1,) * (len(extent) - 1 - dim))
    return gain


def scatter_about(rng, extent, deviation, most, cuts=(), held_as=jnp.bfloat16):
    values = jax.random.normal(rng, extent, jnp.float32) * deviation
    if len(cuts) > 0:
        values = block_levels(rng, extent, cuts, -0.22, 0.18) * values
    return jnp.clip(values, min=-most, max=most).astype(held_as)


def setup_inputs(seed: int = 0) -> dict:
    seeds = jax.random.split(jax.random.key(seed), 5)
    activations = draw_activations(jax.random.fold_in(seeds[4], 71), 0)
    cotangent = scatter_about(seeds[1], (SAMPLES, HGT, WID, D), 1.0, 6.0, ((0, 4), (1, 64)))
    qkv_weight = draw_qkv_weight(jax.random.fold_in(seeds[4], 71), 0)
    out_weight = scatter_about(seeds[3], (D, D), D ** -0.5, 0.21875)
    return dict(activations=activations, cotangent=cotangent, qkv_weight=qkv_weight, out_weight=out_weight)


EPSILON = 1e-06

def rounded(value):
    return lax.optimization_barrier(value.astype(jnp.bfloat16)).astype(jnp.float32)

def attend_block(inputs, cot_block, qkv_weight, out_weight):
    blocks, rows, width = inputs.shape
    as_float = inputs.astype(jnp.float32)
    inverse = lax.rsqrt(lax.optimization_barrier(jnp.mean(as_float * as_float, axis=-1, keepdims=True)) + EPSILON)
    normed = (as_float * inverse).astype(jnp.bfloat16)
    flat_normed = normed.reshape(-1, width)
    projected = rounded(jnp.dot(flat_normed, qkv_weight, preferred_element_type=jnp.float32))
    projected = projected.reshape(blocks, rows, 3, HEADS, HD)
    queries = projected[:, :, 0]
    key_rows = projected[:, :, 1]
    value_rows = projected[:, :, 2]
    scale_factor = HD ** (-0.5)
    scores = jnp.einsum('cinh,cjnh->cnij', queries, key_rows) * scale_factor
    attn_prob = jax.nn.softmax(scores, axis=-1)
    prob_bf = rounded(attn_prob)
    mixed = jnp.einsum('cnij,cjnh->cinh', prob_bf, value_rows)
    mixed_bf = mixed.astype(jnp.bfloat16).reshape(-1, width)
    flat_cot = cot_block.reshape(-1, width)
    grad_mixed = rounded(jnp.dot(flat_cot, out_weight.T, preferred_element_type=jnp.float32))
    grad_mixed = grad_mixed.reshape(blocks, rows, HEADS, HD)
    out_grad = jnp.dot(mixed_bf.T, flat_cot, preferred_element_type=jnp.float32)
    grad_prob = jnp.einsum('cinh,cjnh->cnij', grad_mixed, value_rows)
    grad_score = rounded(attn_prob * (grad_prob - lax.optimization_barrier(jnp.sum(attn_prob * grad_prob, axis=-1, keepdims=True))) * scale_factor)
    grad_query = jnp.einsum('cnij,cjnh->cinh', grad_score, key_rows)
    grad_key = jnp.einsum('cnij,cinh->cjnh', grad_score, queries)
    grad_value = jnp.einsum('cnij,cinh->cjnh', prob_bf, grad_mixed)
    grad_proj = jnp.stack([grad_query, grad_key, grad_value], axis=2).astype(jnp.bfloat16).reshape(-1, 3 * width)
    qkv_grad = jnp.dot(flat_normed.T, grad_proj, preferred_element_type=jnp.float32)
    grad_normed = jnp.dot(grad_proj, qkv_weight.T, preferred_element_type=jnp.float32).reshape(blocks, rows, width)
    centre = lax.optimization_barrier(jnp.mean(grad_normed * as_float, axis=-1, keepdims=True))
    branch = (inverse * grad_normed - as_float * inverse * inverse * inverse * centre).astype(jnp.bfloat16)
    return (branch, qkv_grad, out_grad)

def reference(activations, cotangent, qkv_weight, out_weight):
    column_block = 16
    by_column = activations.transpose(0, 2, 1, 3).reshape(-1, column_block, HGT, D)
    cot_column = cotangent.transpose(0, 2, 1, 3).reshape(-1, column_block, HGT, D)

    def scan_step(carry, column_pair):
        branch, qkv_part, out_part = attend_block(column_pair[0], column_pair[1], qkv_weight, out_weight)
        return ((carry[0] + qkv_part, carry[1] + out_part), branch)
    initial = (jnp.zeros((D, 3 * D), jnp.float32), jnp.zeros((D, D), jnp.float32))
    totals, branches = lax.scan(scan_step, initial, (by_column, cot_column))
    branches = branches.reshape(SAMPLES, WID, HGT, D).transpose(0, 2, 1, 3)
    grads_in = (cotangent.astype(jnp.float32) + branches.astype(jnp.float32)).astype(jnp.bfloat16)
    inverse_root = 1.0 / math.sqrt(SAMPLES * HGT * WID)
    return (grads_in, totals[0] * inverse_root, totals[1] * inverse_root)
```

```python
import functools
import math

import jax
import jax.numpy as jnp
import numpy as np
from jax import lax
from jax.experimental import pallas as pl
from jax.experimental.pallas import tpu as pltpu
from jax.sharding import PartitionSpec as P

HEADS = 12
HD = 64
EPSILON = 1e-06
MESH = pl.DeviceIdType.MESH
BF = jnp.bfloat16
F32 = jnp.float32
GROUP = 2


def one_hot(rows, cols, index):
    o = lax.broadcasted_iota(jnp.int32, (rows, cols), 0)
    i = lax.broadcasted_iota(jnp.int32, (rows, cols), 1)
    return jnp.where(index(o) == i, 1.0, 0.0).astype(BF)


def dot(a, b, ca=1, cb=0):
    return lax.dot_general(a, b, (((ca,), (cb,)), ((), ())), preferred_element_type=F32)


def place():
    band = lax.axis_index("band")
    batch = lax.axis_index("batch")
    return band, batch, band // 16, (band // 4) % 4, band % 4, batch // 2, batch % 2


def band_peer(k, y, zh, x):
    return ((y + k // 16) % 4) * 16 + ((zh + (k // 4) % 4) % 4) * 4 + (x + k % 4) % 4


def exchange_in(act_ref, cot_ref, x_ref, c_ref, send, recv, ssem, rsem):
    band, batch, y, zh, x, zl, core = place()
    barrier = pltpu.get_barrier_semaphore()

    def greet(k, _):
        pl.semaphore_signal(barrier, 1, device_id=(band_peer(k, y, zh, x), batch), device_id_type=MESH)
        return 0

    lax.fori_loop(1, 64, greet, 0)
    perm = one_hot(256, 256, lambda o: ((o & 15) >> 2) * 64 + (o >> 4) * 4 + (o & 3))
    for g in range(4):
        rows = pl.ds(g * 64, 64)
        stack = jnp.concatenate(
            [act_ref[rows, :384], act_ref[rows, 384:], cot_ref[rows, :384], cot_ref[rows, 384:]], axis=0
        )
        send[pl.ds(g * 16, 16)] = dot(perm, stack).astype(BF).reshape(16, 16, 384)
    pl.semaphore_wait(barrier, 63)

    def push(k, _):
        peer = band_peer(k, y, zh, x)
        pltpu.make_async_remote_copy(
            src_ref=send.at[peer],
            dst_ref=recv.at[band],
            send_sem=ssem,
            recv_sem=rsem,
            device_id=(peer, batch),
            device_id_type=MESH,
        ).start()
        return 0

    lax.fori_loop(1, 64, push, 0)
    recv[band] = send[band]
    pltpu.make_async_copy(recv.at[pl.ds(0, 63)], recv.at[pl.ds(0, 63)], rsem).wait()
    back = one_hot(256, 256, lambda o: ((o & 15) << 4) + ((o >> 6) << 2) + ((o >> 4) & 3))
    for blk in range(4):
        got = recv[pl.ds(blk * 16, 16)].reshape(256, 384)
        out = dot(back, got).astype(BF)
        for t in range(4):
            rows = pl.ds(t * 64 + blk * 16, 16)
            x_ref[rows, :384] = out[t * 16 : t * 16 + 16]
            x_ref[rows, 384:] = out[64 + t * 16 : 64 + t * 16 + 16]
            c_ref[rows, :384] = out[128 + t * 16 : 128 + t * 16 + 16]
            c_ref[rows, 384:] = out[192 + t * 16 : 192 + t * 16 + 16]
    pltpu.make_async_copy(send.at[pl.ds(0, 63)], send.at[pl.ds(0, 63)], ssem).wait()


def attend(x_ref, c_ref, wqkv_ref, wout_ref, normed_ref, gp_ref, mixed_ref, branch_ref, proj, gm):
    as_float = x_ref[...].astype(F32)
    inverse = lax.rsqrt(jnp.mean(as_float * as_float, axis=-1, keepdims=True) + EPSILON)
    normed_ref[...] = (as_float * inverse).astype(BF)
    proj[...] = dot(normed_ref[...], wqkv_ref[...]).astype(BF)
    gm[...] = dot(c_ref[...], wout_ref[...], 1, 1).astype(BF)
    scale = HD ** (-0.5)
    wide = GROUP * HD
    lane = lax.broadcasted_iota(jnp.int32, (1, wide), 1) // HD
    masks = [lane == g for g in range(GROUP)]

    def spread(v):
        zero = jnp.zeros_like(v)
        return jnp.concatenate([jnp.where(m, v, zero) for m in masks], axis=0)

    def gather(r):
        out = r[0:64]
        for g in range(1, GROUP):
            out = jnp.where(masks[g], r[g * 64 : g * 64 + 64], out)
        return out

    for c in range(4):
        rows = pl.ds(c * 64, 64)
        for h in range(HEADS // GROUP):
            at = h * wide
            q = proj[rows, at : at + wide]
            k = proj[rows, 768 + at : 768 + at + wide]
            v = proj[rows, 1536 + at : 1536 + at + wide]
            g = gm[rows, at : at + wide]
            qs, gs = spread(q), spread(g)
            s = dot(k, qs, 1, 1) * scale
            e = jnp.exp(s - jnp.max(s, axis=0, keepdims=True))
            p = e / jnp.sum(e, axis=0, keepdims=True)
            pb = p.astype(BF)
            dp = dot(v, gs, 1, 1)
            ds = (p * (dp - jnp.sum(p * dp, axis=0, keepdims=True)) * scale).astype(BF)
            mixed_ref[rows, at : at + wide] = gather(dot(pb, v, 0, 0)).astype(BF)
            gp_ref[rows, at : at + wide] = gather(dot(ds, k, 0, 0)).astype(BF)
            gp_ref[rows, 768 + at : 768 + at + wide] = dot(ds, qs).astype(BF)
            gp_ref[rows, 1536 + at : 1536 + at + wide] = dot(pb, gs).astype(BF)
    gn = dot(gp_ref[...], wqkv_ref[...], 1, 1)
    xf = x_ref[...].astype(F32)
    centre = jnp.mean(gn * xf, axis=-1, keepdims=True)
    branch_ref[...] = (inverse * gn - xf * (inverse * inverse * inverse * centre)).astype(BF)


def reduce_out(
    normed_ref, gp_ref, mixed_ref, ccol_ref, branch_ref, cot_ref, order_ref,
    gin_ref, gqkv_ref, gout_ref,
    nfull, mfull, ghalf, chalf, bsend, brecv, ga, gb, ra, rb, sa, sb, ra2, rb2, tz, rz, tl, rl, tc, rc,
    fsend, frecv, bssem, brsem, ssem, rsem,
):
    band, batch, y, zh, x, zl, core = place()
    barrier = pltpu.get_barrier_semaphore()
    other = (band, zl * 2 + 1 - core)
    across = (band, (1 - zl) * 2 + core)

    def greet(k, _):
        pl.semaphore_signal(barrier, 1, device_id=(band_peer(k, y, zh, x), batch), device_id_type=MESH)
        return 0

    lax.fori_loop(1, 64, greet, 0)
    pl.semaphore_signal(barrier, 1, device_id=other, device_id_type=MESH)
    pl.semaphore_signal(barrier, 1, device_id=across, device_id_type=MESH)
    perm = one_hot(256, 192, lambda o: jnp.where((o & 15) < 12, ((o & 15) >> 2) * 64 + (o & 3) * 16 + (o >> 4), -1))
    for blk in range(4):
        stack = jnp.concatenate(
            [branch_ref[pl.ds(t * 64 + blk * 16, 16), p * 256 : p * 256 + 256] for p in range(3) for t in range(4)],
            axis=0,
        )
        bsend[pl.ds(blk * 16, 16)] = dot(perm, stack).astype(BF).reshape(16, 16, 256)
    pl.semaphore_wait(barrier, 65)

    mine = pl.ds(pl.multiple_of(core * 256, 256), 256)
    theirs_q = pl.ds(pl.multiple_of((1 - core) * 1152, 128), 1152)
    theirs_c = pl.ds(pl.multiple_of((1 - core) * 384, 128), 384)
    own_q = pl.ds(pl.multiple_of(core * 1152, 128), 1152)
    own_c = pl.ds(pl.multiple_of(core * 384, 128), 384)

    def remote(src, dst, s, r, to):
        return pltpu.make_async_remote_copy(
            src_ref=src, dst_ref=dst, send_sem=s, recv_sem=r, device_id=to, device_id_type=MESH
        )

    factors = [
        remote(normed_ref, nfull.at[mine], fsend.at[0], frecv.at[0], other),
        remote(gp_ref.at[:, theirs_q], ghalf.at[mine], fsend.at[1], frecv.at[1], other),
        remote(mixed_ref, mfull.at[mine], fsend.at[2], frecv.at[2], other),
        remote(ccol_ref.at[:, theirs_c], chalf.at[mine], fsend.at[3], frecv.at[3], other),
    ]
    for f in factors:
        f.start()

    def push(k, _):
        peer = band_peer(k, y, zh, x)
        remote(bsend.at[peer], brecv.at[band], bssem, brsem, (peer, batch)).start()
        return 0

    lax.fori_loop(1, 64, push, 0)
    brecv[band] = bsend[band]
    nfull[mine] = normed_ref[...]
    ghalf[mine] = gp_ref[:, own_q]
    mfull[mine] = mixed_ref[...]
    chalf[mine] = ccol_ref[:, own_c]
    for f in factors:
        f.wait()
    nt = dot(order_ref[...], nfull[...], 1, 1).astype(BF)
    mt = dot(order_ref[...], mfull[...], 1, 1).astype(BF)
    for i in range(4):
        q = dot(nt[i * 192 : i * 192 + 192], ghalf[...]).astype(BF)
        o = dot(mt[i * 192 : i * 192 + 192], chalf[...]).astype(BF)
        for j in range(4):
            ga[j, i] = q[j * 48 : j * 48 + 48, :768]
            gb[i, j, :, :384] = q[j * 48 : j * 48 + 48, 768:]
            gb[i, j, :, 384:] = o[j * 48 : j * 48 + 48]

    def x_peer(d):
        return (y * 16 + zh * 4 + (x + d) % 4, batch)

    def y_peer(d):
        return (((y + d) % 4) * 16 + zh * 4 + x, batch)

    def z_peer(d):
        return (y * 16 + ((zh + d) % 4) * 4 + x, batch)

    copies = []
    for d in range(1, 4):
        copies.append(remote(ga.at[(x + d) % 4], ra.at[d - 1], ssem.at[d - 1], rsem.at[d - 1], x_peer(d)))
        copies.append(remote(gb.at[(y + d) % 4], rb.at[d - 1], ssem.at[d + 2], rsem.at[d + 2], y_peer(d)))
    for c in copies:
        c.start()
    for c in copies:
        c.wait_recv()

    def total(own, got):
        t = own.astype(F32)
        for d in range(3):
            t = t + got[d].astype(F32)
        return t

    sa[...] = total(ga[x], ra).astype(BF)
    sb[...] = total(gb[y], rb).astype(BF)
    second = []
    for d in range(1, 4):
        second.append(remote(sa.at[(y + d) % 4], ra2.at[d - 1], ssem.at[d + 5], rsem.at[d + 5], y_peer(d)))
        second.append(remote(sb.at[(x + d) % 4], rb2.at[d - 1], ssem.at[d + 8], rsem.at[d + 8], x_peer(d)))
    for c in second:
        c.start()
    for c in second:
        c.wait_recv()
    pad = one_hot(64, 48, lambda o: jnp.where((o & 15) < 12, (o >> 4) * 12 + (o & 15), -1))
    tz[:, :, :768] = dot(pad, total(sa[y], ra2).astype(BF)).astype(BF).reshape(4, 16, 768)
    tz[:, :, 768:] = dot(pad, total(sb[x], rb2).astype(BF)).astype(BF).reshape(4, 16, 768)
    third = [
        remote(tz.at[(zh + d) % 4], rz.at[d - 1], ssem.at[d + 11], rsem.at[d + 11], z_peer(d)) for d in range(1, 4)
    ]
    for c in third:
        c.start()
    for c in third:
        c.wait_recv()
    tl[...] = total(tz[zh], rz).astype(BF)
    fourth = remote(tl, rl, ssem.at[15], rsem.at[15], across)
    fourth.start()
    pltpu.make_async_copy(brecv.at[pl.ds(0, 63)], brecv.at[pl.ds(0, 63)], brsem).wait()
    back = one_hot(192, 256, lambda o: (((o & 63) >> 2) << 4) + ((o >> 6) << 2) + (o & 3))
    for blk in range(4):
        rows = pl.ds(blk * 64, 64)
        got = dot(back, brecv[pl.ds(blk * 16, 16)].reshape(256, 256))
        for p in range(3):
            at = slice(p * 256, p * 256 + 256)
            gin_ref[rows, at] = (cot_ref[rows, at].astype(F32) + got[p * 64 : p * 64 + 64]).astype(BF)
    fourth.wait_recv()
    tc[...] = (tl[...].astype(F32) + rl[...].astype(F32)) * (1.0 / 256.0)
    fifth = remote(tc, rc, ssem.at[16], rsem.at[16], other)
    fifth.start()
    fifth.wait_recv()
    first = jnp.where(core == 0, tc[...], rc[...])
    last = jnp.where(core == 0, rc[...], tc[...])
    gqkv_ref[:, :1152] = first[:12, :1152]
    gqkv_ref[:, 1152:] = last[:12, :1152]
    gout_ref[:, :384] = first[:12, 1152:]
    gout_ref[:, 384:] = last[:12, 1152:]
    for c in copies + second + third + [fourth, fifth]:
        c.wait_send()
    pltpu.make_async_copy(bsend.at[pl.ds(0, 63)], bsend.at[pl.ds(0, 63)], bssem).wait()


VM = pl.BlockSpec(memory_space=pltpu.VMEM)


def params(cid=None, mib=40):
    if cid is None:
        return pltpu.CompilerParams(vmem_limit_bytes=mib << 20)
    return pltpu.CompilerParams(collective_id=cid, has_side_effects=True, vmem_limit_bytes=mib << 20)


def row_order():
    o = np.arange(768)
    yy, xx, zz, i = o // 192, (o // 48) % 4, (o // 12) % 4, o % 12
    m = np.zeros((768, 768), np.float32)
    m[o, yy * 192 + zz * 48 + xx * 12 + i] = 1.0
    return m


def local(activations, cotangent, qkv_weight, out_weight):
    act = activations.reshape(256, 768)
    cot = cotangent.reshape(256, 768)
    tokens = jax.ShapeDtypeStruct((256, 768), BF)
    xcol, ccol = pl.pallas_call(
        exchange_in,
        out_shape=(tokens, tokens),
        in_specs=[VM, VM],
        out_specs=(VM, VM),
        scratch_shapes=[
            pltpu.VMEM((64, 16, 384), BF),
            pltpu.VMEM((64, 16, 384), BF),
            pltpu.SemaphoreType.DMA,
            pltpu.SemaphoreType.DMA,
        ],
        compiler_params=params(0),
        name="exchange_in",
    )(act, cot)
    normed, gp, mixed, branch = pl.pallas_call(
        attend,
        out_shape=(tokens, jax.ShapeDtypeStruct((256, 2304), BF), tokens, tokens),
        in_specs=[VM] * 4,
        out_specs=(VM,) * 4,
        scratch_shapes=[pltpu.VMEM((256, 2304), BF), pltpu.VMEM((256, 768), BF)],
        compiler_params=params(),
        name="attend",
    )(xcol, ccol, qkv_weight, out_weight)
    order = jnp.asarray(row_order(), dtype=BF)
    gin, gqkv, gout = pl.pallas_call(
        reduce_out,
        out_shape=(tokens, jax.ShapeDtypeStruct((12, 2304), F32), jax.ShapeDtypeStruct((12, 768), F32)),
        in_specs=[VM] * 7,
        out_specs=(VM,) * 3,
        scratch_shapes=[
            pltpu.VMEM((512, 768), BF),
            pltpu.VMEM((512, 768), BF),
            pltpu.VMEM((512, 1152), BF),
            pltpu.VMEM((512, 384), BF),
            pltpu.VMEM((64, 16, 256), BF),
            pltpu.VMEM((64, 16, 256), BF),
            pltpu.VMEM((4, 4, 48, 768), BF),
            pltpu.VMEM((4, 4, 48, 768), BF),
            pltpu.VMEM((3, 4, 48, 768), BF),
            pltpu.VMEM((3, 4, 48, 768), BF),
            pltpu.VMEM((4, 48, 768), BF),
            pltpu.VMEM((4, 48, 768), BF),
            pltpu.VMEM((3, 48, 768), BF),
            pltpu.VMEM((3, 48, 768), BF),
            pltpu.VMEM((4, 16, 1536), BF),
            pltpu.VMEM((3, 16, 1536), BF),
            pltpu.VMEM((16, 1536), BF),
            pltpu.VMEM((16, 1536), BF),
            pltpu.VMEM((16, 1536), F32),
            pltpu.VMEM((16, 1536), F32),
            pltpu.SemaphoreType.DMA((4,)),
            pltpu.SemaphoreType.DMA((4,)),
            pltpu.SemaphoreType.DMA,
            pltpu.SemaphoreType.DMA,
            pltpu.SemaphoreType.DMA((17,)),
            pltpu.SemaphoreType.DMA((17,)),
        ],
        compiler_params=params(1),
        name="reduce_out",
    )(normed, gp, mixed, ccol, branch, cot, order)
    return gin.reshape(activations.shape), gqkv, gout


def solution(mesh):
    return jax.shard_map(
        local,
        mesh=mesh,
        in_specs=(P("batch", "band", None, None), P("batch", "band", None, None), P(), P()),
        out_specs=(P("batch", "band", None, None), P("band", None), P("band", None)),
        check_vma=False,
    )
```

```python
import functools

import jax
import jax.numpy as jnp
import numpy as np
from jax import lax
from jax.experimental import pallas as pl
from jax.experimental.pallas import tpu as pltpu
from jax.sharding import PartitionSpec as P

HEADS = 12
HD = 64
EPSILON = 1e-06
MESH = pl.DeviceIdType.MESH
BF = jnp.bfloat16
F32 = jnp.float32
GROUP = 4
WIDE = GROUP * HD
PAIRS = HEADS // GROUP
BATCH = 6


def one_hot(rows, cols, index):
    o = lax.broadcasted_iota(jnp.int32, (rows, cols), 0)
    i = lax.broadcasted_iota(jnp.int32, (rows, cols), 1)
    return jnp.where(index(o) == i, 1.0, 0.0).astype(BF)


def dot(a, b, ca=1, cb=0):
    return lax.dot_general(a, b, (((ca,), (cb,)), ((), ())), preferred_element_type=F32)


def remote(src, dst, s, r, to):
    return pltpu.make_async_remote_copy(
        src_ref=src, dst_ref=dst, send_sem=s, recv_sem=r, device_id=to, device_id_type=MESH
    )


def body(
    act_hbm, cot_hbm, wqkv_hbm, wout_hbm, ordx_hbm, ordy_hbm,
    gin_hbm, gqkv_hbm, gout_hbm,
    gin_ref, gqkv_ref, gout_ref, out_sem,
    act, cot, wqkv, wout, ordx, ordy,
    send, recv, bsend, brecv,
    x_ref, c_ref, normed, proj, gm, gp, mixed, prob,
    nfx, nfy, mfx, cfull, gfull,
    grad, ring, summed, second, padded, zin, fin,
    load_sem, a2a_s, a2a_r, fac_s, fac_r, ring_s, ring_r, sec_s, sec_r, z_s, z_r, fin_s, fin_r,
):
    band = lax.axis_index("band")
    batch = lax.axis_index("batch")
    y, zh, x = band // 16, (band // 4) % 4, band % 4
    zl, core = batch // 2, batch % 2
    z = zh * 2 + zl

    def peer_of(k):
        return ((y + k // 16) % 4) * 16 + ((zh + (k // 4) % 4) % 4) * 4 + (x + k % 4) % 4

    def at_x(d):
        return (y * 16 + zh * 4 + (x + d) % 4, batch)

    def at_y(d):
        return (((y + d) % 4) * 16 + zh * 4 + x, batch)

    def at_z(d):
        t = (z + d) % 8
        return (y * 16 + (t // 2) * 4 + x, (t % 2) * 2 + core)

    other = (band, zl * 2 + 1 - core)
    across = (band, (1 - zl) * 2 + core)
    corner = (band, (1 - zl) * 2 + 1 - core)

    loads = [
        pltpu.make_async_copy(src, dst, load_sem.at[i])
        for i, (src, dst) in enumerate(
            [(act_hbm, act), (cot_hbm, cot), (wqkv_hbm, wqkv), (ordx_hbm, ordx), (ordy_hbm, ordy), (wout_hbm, wout)]
        )
    ]
    for c in loads:
        c.start()
    barrier = pltpu.get_barrier_semaphore()

    def greet(k, _):
        pl.semaphore_signal(barrier, 1, device_id=(peer_of(k), batch), device_id_type=MESH)
        return 0

    lax.fori_loop(1, 64, greet, 0)
    pl.semaphore_signal(barrier, 1, device_id=other, device_id_type=MESH)
    pl.semaphore_signal(barrier, 1, device_id=corner, device_id_type=MESH)
    for d in (1, 3, 5, 7):
        pl.semaphore_signal(barrier, 1, device_id=at_z(d), device_id_type=MESH)

    fill = one_hot(128, 128, lambda o: ((o >> 2) & 1) * 64 + (o >> 3) * 4 + (o & 3))

    def pack(src, slot):
        for g in range(4):
            rows = pl.ds(g * 64, 64)
            stack = jnp.concatenate([src[rows, :384], src[rows, 384:]], axis=0)
            send[slot, pl.ds(g * 16, 16)] = dot(fill, stack).astype(BF).reshape(16, 8, 384)

    def push(group, src, dst, s, r):
        def one(dz, k):
            peer = ((y + k // 4) % 4) * 16 + ((zh + dz) % 4) * 4 + (x + k % 4) % 4
            pltpu.make_async_remote_copy(
                src_ref=src.at[peer],
                dst_ref=dst.at[band],
                send_sem=s.at[group],
                recv_sem=r.at[group],
                device_id=(peer, batch),
                device_id_type=MESH,
            ).start()

        def far(k, _):
            one(2, k)
            return 0

        def near(k, _):
            one(1, k)
            one(3, k)
            return 0

        def plane(k, _):
            one(0, k)
            return 0

        if group == 0:
            lax.fori_loop(0, 16, far, 0)
        elif group == 1:
            lax.fori_loop(0, 16, near, 0)
        else:
            lax.fori_loop(1, 16, plane, 0)
            dst[band] = src[band]

    def arrive(group, dst, sem):
        n = (16, 32, 15)[group]
        pltpu.make_async_copy(dst.at[pl.ds(0, n)], dst.at[pl.ds(0, n)], sem.at[group]).wait()

    loads[0].wait()
    pack(act, 0)
    pl.semaphore_wait(barrier, 69)
    for g in range(3):
        push(g, send.at[0], recv.at[0], a2a_s.at[0], a2a_r.at[0])
    loads[1].wait()
    pack(cot, 1)
    arrive(0, recv.at[0], a2a_r.at[0])
    for g in range(3):
        push(g, send.at[1], recv.at[1], a2a_s.at[1], a2a_r.at[1])

    empty = one_hot(128, 128, lambda o: ((o & 15) << 3) + ((o >> 6) << 2) + ((o >> 4) & 3))

    def unpack(slot, dst):
        for blk in range(4):
            got = recv[slot, pl.ds(blk * 16, 16)].reshape(128, 384)
            out = dot(empty, got).astype(BF)
            for t in range(4):
                rows = pl.ds(t * 64 + blk * 16, 16)
                dst[rows, :384] = out[t * 16 : t * 16 + 16]
                dst[rows, 384:] = out[64 + t * 16 : 64 + t * 16 + 16]

    arrive(2, recv.at[0], a2a_r.at[0])
    arrive(1, recv.at[0], a2a_r.at[0])
    unpack(0, x_ref)
    as_float = x_ref[...].astype(F32)
    inverse = lax.rsqrt(jnp.mean(as_float * as_float, axis=-1, keepdims=True) + EPSILON)
    normed[...] = (as_float * inverse).astype(BF)
    loads[2].wait()
    proj[...] = dot(normed[...], wqkv[...]).astype(BF)
    half = pl.ds(pl.multiple_of(core * 256, 256), 256)
    loads[3].wait()
    loads[4].wait()
    nfx[:, half] = dot(ordx[...], normed[...], 1, 1).astype(BF)
    nfy[:, half] = dot(ordy[...], normed[...], 1, 1).astype(BF)
    fx = remote(nfx.at[:, half], nfx.at[:, half], fac_s.at[0], fac_r.at[0], other)
    fy = remote(nfy.at[:, half], nfy.at[:, half], fac_s.at[1], fac_r.at[1], other)
    fx.start()
    fy.start()

    scale = HD ** (-0.5)
    lane = lax.broadcasted_iota(jnp.int32, (1, WIDE), 1) // HD
    masks = [lane == g for g in range(GROUP)]

    def spread(v):
        zero = jnp.zeros_like(v)
        return jnp.concatenate([jnp.where(m, v, zero) for m in masks], axis=0)

    def gather(r):
        out = r[0:64]
        for g in range(1, GROUP):
            out = jnp.where(masks[g], r[g * 64 : g * 64 + 64], out)
        return out

    each = [(c, h) for c in range(4) for h in range(PAIRS)]
    batches = [each[n : n + BATCH] for n in range(0, len(each), BATCH)]

    def take(ref, off, it):
        return [ref[pl.ds(c * 64, 64), off + h * WIDE : off + h * WIDE + WIDE] for c, h in it]

    def put(ref, it, values):
        for (c, h), v in zip(it, values):
            ref[pl.ds(c * 64, 64), h * WIDE : h * WIDE + WIDE] = v

    for it in batches:
        qs = [spread(t) for t in take(proj, 0, it)]
        s = [dot(k, q, 1, 1) * scale for k, q in zip(take(proj, 768, it), qs)]
        e = [jnp.exp(t - jnp.max(t, axis=0, keepdims=True)) for t in s]
        p = [t * (1.0 / jnp.sum(t, axis=0, keepdims=True)) for t in e]
        for (c, h), t in zip(it, p):
            prob[c * PAIRS + h] = t
        put(mixed, it, [gather(dot(t.astype(BF), v, 0, 0)).astype(BF) for t, v in zip(p, take(proj, 1536, it))])
    mfx[:, half] = dot(ordx[...], mixed[...], 1, 1).astype(BF)
    fm = remote(mfx.at[:, half], mfx.at[:, half], fac_s.at[2], fac_r.at[2], other)
    fm.start()

    own_c = pl.ds(pl.multiple_of(core * 384, 128), 384)
    their_c = pl.ds(pl.multiple_of((1 - core) * 384, 128), 384)
    loads[5].wait()
    for g in range(3):
        arrive(g, recv.at[1], a2a_r.at[1])
    unpack(1, c_ref)
    fc = remote(c_ref.at[:, their_c], cfull.at[half], fac_s.at[3], fac_r.at[3], other)
    fc.start()
    cfull[half] = c_ref[:, own_c]
    gm[...] = dot(c_ref[...], wout[...], 1, 1).astype(BF)
    for it in batches:
        gs = [spread(t) for t in take(gm, 0, it)]
        p = [prob[c * PAIRS + h].astype(BF) for c, h in it]
        put(gp.at[2], it, [dot(a, b).astype(BF) for a, b in zip(p, gs)])

    def share(s):
        cp = remote(gp.at[s, :, their_c], gfull.at[s, half], fac_s.at[4 + s], fac_r.at[4 + s], other)
        cp.start()
        gfull[s, half] = gp[s, :, own_c]
        return cp

    fv = share(2)

    def first_axis(m):
        return (x, at_x) if m % 2 == 0 else (y, at_y)

    def second_axis(m):
        return (y, at_y) if m % 2 == 0 else (x, at_x)

    def block(pos, part):
        return pl.ds(pl.multiple_of((pos % 4) * 192 + part * 96, 96), 96)

    def ring_copy(m, i, src, to):
        return remote(src, ring.at[m, i], ring_s.at[m, i], ring_r.at[m, i], to)

    def ring_start(m):
        pos, to = first_axis(m)
        g = grad.at[m]
        cps = [
            ring_copy(m, 0, g.at[block(pos + 2, 0)], to(1)),
            ring_copy(m, 1, g.at[block(pos + 2, 1)], to(3)),
            ring_copy(m, 2, g.at[block(pos + 3, 0)], to(3)),
            ring_copy(m, 3, g.at[block(pos + 1, 1)], to(1)),
        ]
        for c in cps:
            c.start()
        return cps

    def ring_pass(m, cps):
        pos, to = first_axis(m)
        cps[0].wait_recv()
        b = block(pos + 1, 0)
        grad[m, b] = (grad[m, b].astype(F32) + ring[m, 0].astype(F32)).astype(BF)
        cps.append(ring_copy(m, 4, grad.at[m, b], to(1)))
        cps[4].start()
        cps[1].wait_recv()
        b = block(pos + 3, 1)
        grad[m, b] = (grad[m, b].astype(F32) + ring[m, 1].astype(F32)).astype(BF)
        cps.append(ring_copy(m, 5, grad.at[m, b], to(3)))
        cps[5].start()

    def ring_end(m, cps):
        pos, _ = first_axis(m)
        for c in cps[2:]:
            c.wait_recv()
        for part, i, j in ((0, 2, 4), (1, 3, 5)):
            t = grad[m, block(pos, part)].astype(F32) + ring[m, i].astype(F32) + ring[m, j].astype(F32)
            summed[m, pl.ds(part * 96, 96)] = t.astype(BF)

    def row48(pos):
        return pl.ds(pl.multiple_of((pos % 4) * 48, 48), 48)

    def second_start(m):
        pos, to = second_axis(m)
        cps = [
            remote(summed.at[m, row48(pos + d)], second.at[m, d - 1], sec_s.at[m, d - 1], sec_r.at[m, d - 1], to(d))
            for d in (2, 1, 3)
        ]
        for c in cps:
            c.start()
        return cps

    pad = one_hot(64, 48, lambda o: jnp.where((o & 15) < 12, (o >> 4) * 12 + (o & 15), -1))

    def second_end(m, cps):
        pos, _ = second_axis(m)
        for c in cps:
            c.wait_recv()
        t = summed[m, row48(pos)].astype(F32)
        for d in range(3):
            t = t + second[m, d].astype(F32)
        padded[m] = dot(pad, t.astype(BF)).astype(BF).reshape(4, 16, 384)

    def z_start(pair):
        out = []
        for d in (4, 3, 5, 2, 6, 1, 7):
            to = (z + d) % 8
            cp = remote(
                padded.at[pair * 2 + to % 2, to // 2], zin.at[pair, z], z_s.at[pair, d - 1], z_r.at[pair, d - 1], at_z(d)
            )
            cp.start()
            out.append(cp)
        zin[pair, z] = padded[pair * 2 + zl, zh]
        return out

    def z_end(pair, cps):
        for c in cps:
            c.wait_recv()
        t = zin[pair, 0].astype(F32)
        for i in range(1, 8):
            t = t + zin[pair, i].astype(F32)
        fin[pair, batch] = (t * (1.0 / 256.0)).astype(BF)
        out = []
        for i, to in enumerate((other, across, corner)):
            cp = remote(fin.at[pair, batch], fin.at[pair, batch], fin_s.at[pair, i], fin_r.at[pair, i], to)
            cp.start()
            out.append(cp)
        return out

    fm.wait_recv()
    fc.wait_recv()
    grad[0] = dot(mfx[...], cfull[...]).astype(BF)
    r0 = ring_start(0)
    fy.wait_recv()
    fv.wait_recv()
    grad[1] = dot(nfy[...], gfull[2]).astype(BF)
    r1 = ring_start(1)
    for it in batches:
        gs = [spread(t) for t in take(gm, 0, it)]
        dp = [dot(v, g, 1, 1) for v, g in zip(take(proj, 1536, it), gs)]
        p = [prob[c * PAIRS + h] for c, h in it]
        ds = [(a * (d - jnp.sum(a * d, axis=0, keepdims=True)) * scale).astype(BF) for a, d in zip(p, dp)]
        put(gp.at[0], it, [gather(dot(d, k, 0, 0)).astype(BF) for d, k in zip(ds, take(proj, 768, it))])
        qs = [spread(t) for t in take(proj, 0, it)]
        put(gp.at[1], it, [dot(d, q).astype(BF) for d, q in zip(ds, qs)])
    fq = share(0)
    fk = share(1)
    ring_pass(0, r0)
    ring_pass(1, r1)
    fx.wait_recv()
    fq.wait_recv()
    grad[2] = dot(nfx[...], gfull[0]).astype(BF)
    r2 = ring_start(2)
    fk.wait_recv()
    grad[3] = dot(nfy[...], gfull[1]).astype(BF)
    r3 = ring_start(3)
    gn = dot(gp[0], wqkv[:, :768], 1, 1) + dot(gp[1], wqkv[:, 768:1536], 1, 1) + dot(gp[2], wqkv[:, 1536:], 1, 1)
    xf = x_ref[...].astype(F32)
    centre = jnp.mean(gn * xf, axis=-1, keepdims=True)
    branch = (inverse * gn - xf * (inverse * inverse * inverse * centre)).astype(BF)
    back = one_hot(128, 128, lambda o: ((o >> 2) & 1) * 64 + (o & 3) * 16 + (o >> 3))
    for blk in range(4):
        stack = jnp.concatenate(
            [branch[t * 64 + blk * 16 : t * 64 + blk * 16 + 16, p * 384 : p * 384 + 384] for p in range(2) for t in range(4)],
            axis=0,
        )
        bsend[pl.ds(blk * 16, 16)] = dot(back, stack).astype(BF).reshape(16, 8, 384)
    ring_pass(2, r2)
    ring_pass(3, r3)
    for g in range(3):
        push(g, bsend, brecv, a2a_s.at[2], a2a_r.at[2])
    ring_end(0, r0)
    s0 = second_start(0)
    ring_end(1, r1)
    s1 = second_start(1)
    ring_end(2, r2)
    s2 = second_start(2)
    ring_end(3, r3)
    s3 = second_start(3)
    second_end(0, s0)
    second_end(1, s1)
    z0 = z_start(0)
    second_end(2, s2)
    second_end(3, s3)
    z1 = z_start(1)
    e0 = z_end(0, z0)
    for g in range(3):
        arrive(g, brecv, a2a_r.at[2])
    home = one_hot(128, 128, lambda o: (((o & 63) >> 2) << 3) + ((o >> 6) << 2) + (o & 3))
    for blk in range(4):
        rows = pl.ds(blk * 64, 64)
        got = dot(home, brecv[pl.ds(blk * 16, 16)].reshape(128, 384))
        gin_ref[rows, :384] = (cot[rows, :384].astype(F32) + got[:64]).astype(BF)
        gin_ref[rows, 384:] = (cot[rows, 384:].astype(F32) + got[64:]).astype(BF)
    outs = [
        pltpu.make_async_copy(src, dst, out_sem.at[i])
        for i, (src, dst) in enumerate([(gin_ref, gin_hbm), (gqkv_ref, gqkv_hbm), (gout_ref, gout_hbm)])
    ]
    outs[0].start()
    e1 = z_end(1, z1)
    for pair, cps in ((0, e0), (1, e1)):
        for c in cps:
            c.wait_recv()
        for q in range(4):
            m = pair * 2 + q // 2
            at = (0, 1536, 0, 768)[m] + (q % 2) * 384
            dst = gout_ref if m == 0 else gqkv_ref
            dst[:, at : at + 384] = fin[pair, q].astype(F32)[:12]
    outs[1].start()
    outs[2].start()
    for c in [fx, fy, fm, fc, fv, fq, fk] + r0 + r1 + r2 + r3 + s0 + s1 + s2 + s3 + z0 + z1 + e0 + e1:
        c.wait_send()
    for g in range(3):
        arrive(g, send.at[0], a2a_s.at[0])
        arrive(g, send.at[1], a2a_s.at[1])
        arrive(g, bsend, a2a_s.at[2])
    for c in outs:
        c.wait()


def hand_over(a, b, c, a_out, b_out, c_out, va, vb, vc, sem):
    here = [pltpu.make_async_copy(src, dst, sem.at[i]) for i, (src, dst) in enumerate([(a, va), (b, vb), (c, vc)])]
    away = [
        pltpu.make_async_copy(src, dst, sem.at[i + 3]) for i, (src, dst) in enumerate([(va, a_out), (vb, b_out), (vc, c_out)])
    ]
    for cp in here:
        cp.start()
    for first, then in zip(here, away):
        first.wait()
        then.start()
    for cp in away:
        cp.wait()


def orders():
    o = np.arange(768)
    a, b, c, i = o // 192, (o // 48) % 4, (o // 12) % 4, o % 12
    out = []
    for yy, xx in ((b, a), (a, b)):
        m = np.zeros((768, 768), np.float32)
        m[o, yy * 192 + c * 48 + xx * 12 + i] = 1.0
        out.append(jnp.asarray(m, dtype=BF))
    return out


def local(activations, cotangent, qkv_weight, out_weight):
    act = activations.reshape(256, 768)
    cot = cotangent.reshape(256, 768)
    ordx, ordy = orders()
    vm = pltpu.VMEM
    dma = pltpu.SemaphoreType.DMA
    hbm = pl.BlockSpec(memory_space=pltpu.HBM)
    gin, gqkv, gout = pl.pallas_call(
        body,
        out_shape=(
            jax.ShapeDtypeStruct((256, 768), BF),
            jax.ShapeDtypeStruct((12, 2304), F32),
            jax.ShapeDtypeStruct((12, 768), F32),
        ),
        in_specs=[hbm] * 6,
        out_specs=(hbm,) * 3,
        scratch_shapes=[
            vm((256, 768), BF),
            vm((12, 2304), F32),
            vm((12, 768), F32),
            dma((3,)),
            vm((256, 768), BF),
            vm((256, 768), BF),
            vm((768, 2304), BF),
            vm((768, 768), BF),
            vm((768, 768), BF),
            vm((768, 768), BF),
            vm((2, 64, 8, 384), BF),
            vm((2, 64, 8, 384), BF),
            vm((64, 8, 384), BF),
            vm((64, 8, 384), BF),
            vm((256, 768), BF),
            vm((256, 768), BF),
            vm((256, 768), BF),
            vm((256, 2304), BF),
            vm((256, 768), BF),
            vm((3, 256, 768), BF),
            vm((256, 768), BF),
            vm((4 * PAIRS, 64, WIDE), F32),
            vm((768, 512), BF),
            vm((768, 512), BF),
            vm((768, 512), BF),
            vm((512, 384), BF),
            vm((3, 512, 384), BF),
            vm((4, 768, 384), BF),
            vm((4, 6, 96, 384), BF),
            vm((4, 192, 384), BF),
            vm((4, 3, 48, 384), BF),
            vm((4, 4, 16, 384), BF),
            vm((2, 8, 16, 384), BF),
            vm((2, 4, 16, 384), BF),
            dma((6,)),
            dma((3, 3)),
            dma((3, 3)),
            dma((7,)),
            dma((7,)),
            dma((4, 6)),
            dma((4, 6)),
            dma((4, 3)),
            dma((4, 3)),
            dma((2, 7)),
            dma((2, 7)),
            dma((2, 3)),
            dma((2, 3)),
        ],
        compiler_params=pltpu.CompilerParams(collective_id=0, has_side_effects=True, vmem_limit_bytes=62 << 20),
        name="column_backward",
    )(act, cot, qkv_weight, out_weight, ordx, ordy)
    gin, gqkv, gout = pl.pallas_call(
        hand_over,
        out_shape=tuple(jax.ShapeDtypeStruct(v.shape, v.dtype) for v in (gin, gqkv, gout)),
        in_specs=[hbm] * 3,
        out_specs=(hbm,) * 3,
        scratch_shapes=[vm((256, 768), BF), vm((12, 2304), F32), vm((12, 768), F32), dma((6,))],
        name="hand_over",
    )(gin, gqkv, gout)
    return gin.reshape(activations.shape), gqkv, gout


def solution(mesh):
    return jax.shard_map(
        local,
        mesh=mesh,
        in_specs=(P("batch", "band", None, None), P("batch", "band", None, None), P(), P()),
        out_specs=(P("batch", "band", None, None), P("band", None), P("band", None)),
        check_vma=False,
    )
```

```python
import functools

import jax
import jax.numpy as jnp
import numpy as np
from jax import lax
from jax.experimental import pallas as pl
from jax.experimental.pallas import tpu as pltpu
from jax.sharding import PartitionSpec as P

HEADS = 12
HD = 64
EPSILON = 1e-06
MESH = pl.DeviceIdType.MESH
BF = jnp.bfloat16
F32 = jnp.float32
GROUP = 4
WIDE = GROUP * HD
PAIRS = HEADS // GROUP
DIRECT = ()
BATCH = 6


def one_hot(rows, cols, index):
    o = lax.broadcasted_iota(jnp.int32, (rows, cols), 0)
    i = lax.broadcasted_iota(jnp.int32, (rows, cols), 1)
    return jnp.where(index(o) == i, 1.0, 0.0).astype(BF)


def dot(a, b, ca=1, cb=0):
    return lax.dot_general(a, b, (((ca,), (cb,)), ((), ())), preferred_element_type=F32)


def remote(src, dst, s, r, to):
    return pltpu.make_async_remote_copy(
        src_ref=src, dst_ref=dst, send_sem=s, recv_sem=r, device_id=to, device_id_type=MESH
    )


def body(
    act_hbm, cot_hbm, wqkv_hbm, wout_hbm, ordx_hbm, ordy_hbm,
    gin_hbm, gqkv_hbm, gout_hbm,
    gin_ref, gqkv_ref, gout_ref, out_sem,
    act, cot, wqkv, wout, ordx, ordy,
    send, recv, bsend, brecv,
    x_ref, c_ref, normed, proj, gm, gp, mixed, prob,
    nfx, nfy, mfx, cfull, gfull,
    grad, ring, summed, second, padded, zin, fin,
    plane_in, load_sem, a2a_s, a2a_r, fac_s, fac_r, ring_s, ring_r, sec_s, sec_r, z_s, z_r, fin_s, fin_r,
):
    band = lax.axis_index("band")
    batch = lax.axis_index("batch")
    y, zh, x = band // 16, (band // 4) % 4, band % 4
    zl, core = batch // 2, batch % 2
    z = zh * 2 + zl

    def at_x(d):
        return (y * 16 + zh * 4 + (x + d) % 4, batch)

    def at_y(d):
        return (((y + d) % 4) * 16 + zh * 4 + x, batch)

    def at_z(d):
        t = (z + d) % 8
        return (y * 16 + (t // 2) * 4 + x, (t % 2) * 2 + core)

    other = (band, zl * 2 + 1 - core)
    across = (band, (1 - zl) * 2 + core)
    corner = (band, (1 - zl) * 2 + 1 - core)

    loads = [
        pltpu.make_async_copy(src, dst, load_sem.at[i])
        for i, (src, dst) in enumerate(
            [(act_hbm, act), (cot_hbm, cot), (wqkv_hbm, wqkv), (ordx_hbm, ordx), (ordy_hbm, ordy), (wout_hbm, wout)]
        )
    ]
    loads[0].start()
    barrier = pltpu.get_barrier_semaphore()
    for k in range(1, 16):
        to = ((y + k // 4) % 4) * 16 + zh * 4 + (x + k % 4) % 4
        pl.semaphore_signal(barrier, 1, device_id=(to, batch), device_id_type=MESH)
    for d in range(1, 8):
        pl.semaphore_signal(barrier, 1, device_id=at_z(d), device_id_type=MESH)
    for to in (other, corner):
        pl.semaphore_signal(barrier, 1, device_id=to, device_id_type=MESH)
    for c in loads[1:]:
        c.start()

    fill = one_hot(128, 128, lambda o: ((o >> 2) & 1) * 64 + (o >> 3) * 4 + (o & 3))

    def pack(src, slot):
        for g in range(4):
            rows = pl.ds(g * 64, 64)
            stack = jnp.concatenate([src[rows, :384], src[rows, 384:]], axis=0)
            send[slot, pl.ds(g * 16, 16)] = dot(fill, stack).astype(BF).reshape(16, 8, 384)

    def push(group, src, dst, s, r):
        def one(dz, k):
            peer = ((y + k // 4) % 4) * 16 + ((zh + dz) % 4) * 4 + (x + k % 4) % 4
            pltpu.make_async_remote_copy(
                src_ref=src.at[peer],
                dst_ref=dst.at[band],
                send_sem=s.at[group],
                recv_sem=r.at[group],
                device_id=(peer, batch),
                device_id_type=MESH,
            ).start()

        def far(k, _):
            one(2, k)
            return 0

        def near(k, _):
            one(1, k)
            one(3, k)
            return 0

        def plane(k, _):
            one(0, k)
            return 0

        if group == 0:
            lax.fori_loop(0, 16, far, 0)
        elif group == 1:
            lax.fori_loop(0, 16, near, 0)
        else:
            lax.fori_loop(1, 16, plane, 0)
            dst[band] = src[band]

    def arrive(group, dst, sem):
        n = (16, 32, 15)[group]
        pltpu.make_async_copy(dst.at[pl.ds(0, n)], dst.at[pl.ds(0, n)], sem.at[group]).wait()

    loads[0].wait()
    pack(act, 0)
    pl.semaphore_wait(barrier, 24)
    for d in (2, 4, 6):
        pl.semaphore_signal(plane_in, 1, device_id=at_z(d), device_id_type=MESH)
    pl.semaphore_wait(plane_in, 3)
    for g in range(3):
        push(g, send.at[0], recv.at[0], a2a_s.at[0], a2a_r.at[0])
    loads[1].wait()
    pack(cot, 1)
    for g in range(3):
        push(g, send.at[1], recv.at[1], a2a_s.at[1], a2a_r.at[1])

    empty = one_hot(128, 128, lambda o: ((o & 15) << 3) + ((o >> 6) << 2) + ((o >> 4) & 3))

    def unpack(slot, dst):
        for blk in range(4):
            got = recv[slot, pl.ds(blk * 16, 16)].reshape(128, 384)
            out = dot(empty, got).astype(BF)
            for t in range(4):
                rows = pl.ds(t * 64 + blk * 16, 16)
                dst[rows, :384] = out[t * 16 : t * 16 + 16]
                dst[rows, 384:] = out[64 + t * 16 : 64 + t * 16 + 16]

    arrive(0, recv.at[0], a2a_r.at[0])
    arrive(2, recv.at[0], a2a_r.at[0])
    arrive(1, recv.at[0], a2a_r.at[0])
    unpack(0, x_ref)
    as_float = x_ref[...].astype(F32)
    inverse = lax.rsqrt(jnp.mean(as_float * as_float, axis=-1, keepdims=True) + EPSILON)
    normed[...] = (as_float * inverse).astype(BF)
    loads[2].wait()
    proj[...] = dot(normed[...], wqkv[...]).astype(BF)
    half = pl.ds(pl.multiple_of(core * 256, 256), 256)
    loads[3].wait()
    loads[4].wait()
    nfx[:, half] = dot(ordx[...], normed[...], 1, 1).astype(BF)
    nfy[:, half] = dot(ordy[...], normed[...], 1, 1).astype(BF)
    fx = remote(nfx.at[:, half], nfx.at[:, half], fac_s.at[0], fac_r.at[0], other)
    fy = remote(nfy.at[:, half], nfy.at[:, half], fac_s.at[1], fac_r.at[1], other)
    fx.start()
    fy.start()

    scale = HD ** (-0.5)
    lane = lax.broadcasted_iota(jnp.int32, (1, WIDE), 1) // HD
    masks = [lane == g for g in range(GROUP)]

    def spread(v):
        zero = jnp.zeros_like(v)
        return jnp.concatenate([jnp.where(m, v, zero) for m in masks], axis=0)

    def gather(r):
        out = r[0:64]
        for g in range(1, GROUP):
            out = jnp.where(masks[g], r[g * 64 : g * 64 + 64], out)
        return out

    each = [(c, h) for c in range(4) for h in range(PAIRS)]
    batches = [each[n : n + BATCH] for n in range(0, len(each), BATCH)]

    def take(ref, off, it):
        return [ref[pl.ds(c * 64, 64), off + h * WIDE : off + h * WIDE + WIDE] for c, h in it]

    def put(ref, it, values):
        for (c, h), v in zip(it, values):
            ref[pl.ds(c * 64, 64), h * WIDE : h * WIDE + WIDE] = v

    for it in batches:
        qs = [spread(t) for t in take(proj, 0, it)]
        s = [dot(k, q, 1, 1) * scale for k, q in zip(take(proj, 768, it), qs)]
        e = [jnp.exp(t - jnp.max(t, axis=0, keepdims=True)) for t in s]
        p = [t * (1.0 / jnp.sum(t, axis=0, keepdims=True)) for t in e]
        for (c, h), t in zip(it, p):
            prob[c * PAIRS + h] = t
        put(mixed, it, [gather(dot(t.astype(BF), v, 0, 0)).astype(BF) for t, v in zip(p, take(proj, 1536, it))])
    mfx[:, half] = dot(ordx[...], mixed[...], 1, 1).astype(BF)
    fm = remote(mfx.at[:, half], mfx.at[:, half], fac_s.at[2], fac_r.at[2], other)
    fm.start()

    own_c = pl.ds(pl.multiple_of(core * 384, 128), 384)
    their_c = pl.ds(pl.multiple_of((1 - core) * 384, 128), 384)
    loads[5].wait()
    for g in range(3):
        arrive(g, recv.at[1], a2a_r.at[1])
    unpack(1, c_ref)
    fc = remote(c_ref.at[:, their_c], cfull.at[half], fac_s.at[3], fac_r.at[3], other)
    fc.start()
    cfull[half] = c_ref[:, own_c]
    gm[...] = dot(c_ref[...], wout[...], 1, 1).astype(BF)
    for it in batches:
        gs = [spread(t) for t in take(gm, 0, it)]
        dp = [dot(v, g, 1, 1) for v, g in zip(take(proj, 1536, it), gs)]
        p = [prob[c * PAIRS + h] for c, h in it]
        put(gp.at[2], it, [dot(a.astype(BF), g).astype(BF) for a, g in zip(p, gs)])
        ds = [(a * (d - jnp.sum(a * d, axis=0, keepdims=True)) * scale).astype(BF) for a, d in zip(p, dp)]
        put(gp.at[0], it, [gather(dot(d, k, 0, 0)).astype(BF) for d, k in zip(ds, take(proj, 768, it))])
        qs = [spread(t) for t in take(proj, 0, it)]
        put(gp.at[1], it, [dot(d, q).astype(BF) for d, q in zip(ds, qs)])

    def share(s):
        cp = remote(gp.at[s, :, their_c], gfull.at[s, half], fac_s.at[4 + s], fac_r.at[4 + s], other)
        cp.start()
        gfull[s, half] = gp[s, :, own_c]
        return cp

    fv = share(2)
    fq = share(0)
    fk = share(1)

    def first_axis(m):
        return (x, at_x) if m % 2 == 0 else (y, at_y)

    def second_axis(m):
        return (y, at_y) if m % 2 == 0 else (x, at_x)

    def block(pos, part):
        return pl.ds(pl.multiple_of((pos % 4) * 192 + part * 96, 96), 96)

    def slot(m, i):
        return ring.at[m, i // 2, pl.ds((i % 2) * 96, 96)]

    def ring_copy(m, i, src, to):
        return remote(src, slot(m, i), ring_s.at[m, i], ring_r.at[m, i], to)

    def ring_start(m):
        pos, to = first_axis(m)
        g = grad.at[m]
        if m in DIRECT:
            cps = []
            for d in (2, 1, 3):
                src = g.at[pl.ds(pl.multiple_of((pos + d) % 4 * 192, 192), 192)]
                cps.append(remote(src, ring.at[m, d - 1], ring_s.at[m, d - 1], ring_r.at[m, d - 1], to(d)))
        else:
            cps = [
                ring_copy(m, 0, g.at[block(pos + 2, 0)], to(1)),
                ring_copy(m, 1, g.at[block(pos + 2, 1)], to(3)),
                ring_copy(m, 2, g.at[block(pos + 3, 0)], to(3)),
                ring_copy(m, 3, g.at[block(pos + 1, 1)], to(1)),
            ]
        for c in cps:
            c.start()
        return cps

    def ring_pass(m, cps):
        if m in DIRECT:
            return
        pos, to = first_axis(m)
        cps[0].wait_recv()
        b = block(pos + 1, 0)
        grad[m, b] = (grad[m, b].astype(F32) + slot(m, 0)[...].astype(F32)).astype(BF)
        cps.append(ring_copy(m, 4, grad.at[m, b], to(1)))
        cps[4].start()
        cps[1].wait_recv()
        b = block(pos + 3, 1)
        grad[m, b] = (grad[m, b].astype(F32) + slot(m, 1)[...].astype(F32)).astype(BF)
        cps.append(ring_copy(m, 5, grad.at[m, b], to(3)))
        cps[5].start()

    def ring_end(m, cps):
        pos, _ = first_axis(m)
        if m in DIRECT:
            for c in cps:
                c.wait_recv()
            t = grad[m, pl.ds(pl.multiple_of(pos * 192, 192), 192)].astype(F32)
            for d in range(3):
                t = t + ring[m, d].astype(F32)
            summed[m] = t.astype(BF)
            return
        for c in cps[2:]:
            c.wait_recv()
        for part, i, j in ((0, 2, 4), (1, 3, 5)):
            t = grad[m, block(pos, part)].astype(F32) + slot(m, i)[...].astype(F32) + slot(m, j)[...].astype(F32)
            summed[m, pl.ds(part * 96, 96)] = t.astype(BF)

    def row48(pos):
        return pl.ds(pl.multiple_of((pos % 4) * 48, 48), 48)

    def second_start(m):
        pos, to = second_axis(m)
        cps = [
            remote(summed.at[m, row48(pos + d)], second.at[m, d - 1], sec_s.at[m, d - 1], sec_r.at[m, d - 1], to(d))
            for d in (2, 1, 3)
        ]
        for c in cps:
            c.start()
        return cps

    pad = one_hot(64, 48, lambda o: jnp.where((o & 15) < 12, (o >> 4) * 12 + (o & 15), -1))

    def second_end(m, cps):
        pos, _ = second_axis(m)
        for c in cps:
            c.wait_recv()
        t = summed[m, row48(pos)].astype(F32)
        for d in range(3):
            t = t + second[m, d].astype(F32)
        padded[m] = dot(pad, t.astype(BF)).astype(BF).reshape(4, 16, 384)

    def z_start(pair):
        out = []
        for d in (4, 3, 5, 2, 6, 1, 7):
            to = (z + d) % 8
            cp = remote(
                padded.at[pair * 2 + to % 2, to // 2], zin.at[pair, z], z_s.at[pair, d - 1], z_r.at[pair, d - 1], at_z(d)
            )
            cp.start()
            out.append(cp)
        zin[pair, z] = padded[pair * 2 + zl, zh]
        return out

    def z_end(pair, cps):
        for c in cps:
            c.wait_recv()
        t = zin[pair, 0].astype(F32)
        for i in range(1, 8):
            t = t + zin[pair, i].astype(F32)
        fin[pair, batch] = (t * (1.0 / 256.0)).astype(BF)
        out = []
        for i, to in enumerate((other, across, corner)):
            cp = remote(fin.at[pair, batch], fin.at[pair, batch], fin_s.at[pair, i], fin_r.at[pair, i], to)
            cp.start()
            out.append(cp)
        return out

    fm.wait_recv()
    fc.wait_recv()
    grad[0] = dot(mfx[...], cfull[...]).astype(BF)
    r0 = ring_start(0)
    fy.wait_recv()
    fv.wait_recv()
    grad[1] = dot(nfy[...], gfull[2]).astype(BF)
    r1 = ring_start(1)
    fx.wait_recv()
    fq.wait_recv()
    grad[2] = dot(nfx[...], gfull[0]).astype(BF)
    r2 = ring_start(2)
    fk.wait_recv()
    grad[3] = dot(nfy[...], gfull[1]).astype(BF)
    r3 = ring_start(3)
    ring_pass(0, r0)
    ring_pass(1, r1)
    gn = dot(gp[0], wqkv[:, :768], 1, 1) + dot(gp[1], wqkv[:, 768:1536], 1, 1) + dot(gp[2], wqkv[:, 1536:], 1, 1)
    xf = x_ref[...].astype(F32)
    centre = jnp.mean(gn * xf, axis=-1, keepdims=True)
    branch = (inverse * gn - xf * (inverse * inverse * inverse * centre)).astype(BF)
    back = one_hot(128, 128, lambda o: ((o >> 2) & 1) * 64 + (o & 3) * 16 + (o >> 3))
    for blk in range(4):
        stack = jnp.concatenate(
            [branch[t * 64 + blk * 16 : t * 64 + blk * 16 + 16, p * 384 : p * 384 + 384] for p in range(2) for t in range(4)],
            axis=0,
        )
        bsend[pl.ds(blk * 16, 16)] = dot(back, stack).astype(BF).reshape(16, 8, 384)
    ring_pass(2, r2)
    ring_pass(3, r3)
    for g in range(3):
        push(g, bsend, brecv, a2a_s.at[2], a2a_r.at[2])
    ring_end(0, r0)
    s0 = second_start(0)
    ring_end(1, r1)
    s1 = second_start(1)
    ring_end(2, r2)
    s2 = second_start(2)
    ring_end(3, r3)
    s3 = second_start(3)
    second_end(0, s0)
    second_end(1, s1)
    z0 = z_start(0)
    second_end(2, s2)
    second_end(3, s3)
    z1 = z_start(1)
    e0 = z_end(0, z0)
    for g in range(3):
        arrive(g, brecv, a2a_r.at[2])
    home = one_hot(128, 128, lambda o: (((o & 63) >> 2) << 3) + ((o >> 6) << 2) + (o & 3))
    for blk in range(4):
        rows = pl.ds(blk * 64, 64)
        got = dot(home, brecv[pl.ds(blk * 16, 16)].reshape(128, 384))
        gin_ref[rows, :384] = (cot[rows, :384].astype(F32) + got[:64]).astype(BF)
        gin_ref[rows, 384:] = (cot[rows, 384:].astype(F32) + got[64:]).astype(BF)
    outs = [
        pltpu.make_async_copy(src, dst, out_sem.at[i])
        for i, (src, dst) in enumerate([(gin_ref, gin_hbm), (gqkv_ref, gqkv_hbm), (gout_ref, gout_hbm)])
    ]
    outs[0].start()
    e1 = z_end(1, z1)
    for pair, cps in ((0, e0), (1, e1)):
        for c in cps:
            c.wait_recv()
        for q in range(4):
            m = pair * 2 + q // 2
            at = (0, 1536, 0, 768)[m] + (q % 2) * 384
            dst = gout_ref if m == 0 else gqkv_ref
            dst[:, at : at + 384] = fin[pair, q].astype(F32)[:12]
    outs[1].start()
    outs[2].start()
    for c in [fx, fy, fm, fc, fv, fq, fk] + r0 + r1 + r2 + r3 + s0 + s1 + s2 + s3 + z0 + z1 + e0 + e1:
        c.wait_send()
    for g in range(3):
        arrive(g, send.at[0], a2a_s.at[0])
        arrive(g, send.at[1], a2a_s.at[1])
        arrive(g, bsend, a2a_s.at[2])
    for c in outs:
        c.wait()


def hand_over(a, b, c, a_out, b_out, c_out, va, vb, vc, sem):
    here = [pltpu.make_async_copy(src, dst, sem.at[i]) for i, (src, dst) in enumerate([(a, va), (b, vb), (c, vc)])]
    away = [
        pltpu.make_async_copy(src, dst, sem.at[i + 3]) for i, (src, dst) in enumerate([(va, a_out), (vb, b_out), (vc, c_out)])
    ]
    for cp in here:
        cp.start()
    for first, then in zip(here, away):
        first.wait()
        then.start()
    for cp in away:
        cp.wait()


def orders():
    o = np.arange(768)
    a, b, c, i = o // 192, (o // 48) % 4, (o // 12) % 4, o % 12
    out = []
    for yy, xx in ((b, a), (a, b)):
        m = np.zeros((768, 768), np.float32)
        m[o, yy * 192 + c * 48 + xx * 12 + i] = 1.0
        out.append(jnp.asarray(m, dtype=BF))
    return out


def local(activations, cotangent, qkv_weight, out_weight):
    act = activations.reshape(256, 768)
    cot = cotangent.reshape(256, 768)
    ordx, ordy = orders()
    vm = pltpu.VMEM
    dma = pltpu.SemaphoreType.DMA
    hbm = pl.BlockSpec(memory_space=pltpu.HBM)
    gin, gqkv, gout = pl.pallas_call(
        body,
        out_shape=(
            jax.ShapeDtypeStruct((256, 768), BF),
            jax.ShapeDtypeStruct((12, 2304), F32),
            jax.ShapeDtypeStruct((12, 768), F32),
        ),
        in_specs=[hbm] * 6,
        out_specs=(hbm,) * 3,
        scratch_shapes=[
            vm((256, 768), BF),
            vm((12, 2304), F32),
            vm((12, 768), F32),
            dma((3,)),
            vm((256, 768), BF),
            vm((256, 768), BF),
            vm((768, 2304), BF),
            vm((768, 768), BF),
            vm((768, 768), BF),
            vm((768, 768), BF),
            vm((2, 64, 8, 384), BF),
            vm((2, 64, 8, 384), BF),
            vm((64, 8, 384), BF),
            vm((64, 8, 384), BF),
            vm((256, 768), BF),
            vm((256, 768), BF),
            vm((256, 768), BF),
            vm((256, 2304), BF),
            vm((256, 768), BF),
            vm((3, 256, 768), BF),
            vm((256, 768), BF),
            vm((4 * PAIRS, 64, WIDE), F32),
            vm((768, 512), BF),
            vm((768, 512), BF),
            vm((768, 512), BF),
            vm((512, 384), BF),
            vm((3, 512, 384), BF),
            vm((4, 768, 384), BF),
            vm((4, 3, 192, 384), BF),
            vm((4, 192, 384), BF),
            vm((4, 3, 48, 384), BF),
            vm((4, 4, 16, 384), BF),
            vm((2, 8, 16, 384), BF),
            vm((2, 4, 16, 384), BF),
            pltpu.SemaphoreType.REGULAR,
            dma((6,)),
            dma((3, 3)),
            dma((3, 3)),
            dma((7,)),
            dma((7,)),
            dma((4, 6)),
            dma((4, 6)),
            dma((4, 3)),
            dma((4, 3)),
            dma((2, 7)),
            dma((2, 7)),
            dma((2, 3)),
            dma((2, 3)),
        ],
        compiler_params=pltpu.CompilerParams(collective_id=0, has_side_effects=True, vmem_limit_bytes=62 << 20),
        name="column_backward",
    )(act, cot, qkv_weight, out_weight, ordx, ordy)
    gin, gqkv, gout = pl.pallas_call(
        hand_over,
        out_shape=tuple(jax.ShapeDtypeStruct(v.shape, v.dtype) for v in (gin, gqkv, gout)),
        in_specs=[hbm] * 3,
        out_specs=(hbm,) * 3,
        scratch_shapes=[vm((256, 768), BF), vm((12, 2304), F32), vm((12, 768), F32), dma((6,))],
        name="hand_over",
    )(gin, gqkv, gout)
    return gin.reshape(activations.shape), gqkv, gout


def solution(mesh):
    return jax.shard_map(
        local,
        mesh=mesh,
        in_specs=(P("batch", "band", None, None), P("batch", "band", None, None), P(), P()),
        out_specs=(P("batch", "band", None, None), P("band", None), P("band", None)),
        check_vma=False,
    )
```

```python
import functools

import jax
import jax.numpy as jnp
import numpy as np
from jax import lax
from jax.experimental import pallas as pl
from jax.experimental.pallas import tpu as pltpu
from jax.sharding import PartitionSpec as P

HEADS = 12
HD = 64
EPSILON = 1e-06
MESH = pl.DeviceIdType.MESH
BF = jnp.bfloat16
F32 = jnp.float32
GROUP = 4
WIDE = GROUP * HD
PAIRS = HEADS // GROUP
BATCH = 6


def one_hot(rows, cols, index):
    o = lax.broadcasted_iota(jnp.int32, (rows, cols), 0)
    i = lax.broadcasted_iota(jnp.int32, (rows, cols), 1)
    return jnp.where(index(o) == i, 1.0, 0.0).astype(BF)


def dot(a, b, ca=1, cb=0):
    return lax.dot_general(a, b, (((ca,), (cb,)), ((), ())), preferred_element_type=F32)


def remote(src, dst, s, r, to):
    return pltpu.make_async_remote_copy(
        src_ref=src, dst_ref=dst, send_sem=s, recv_sem=r, device_id=to, device_id_type=MESH
    )


def body(
    act_hbm, cot_hbm, wqkv_hbm, wout_hbm, ordx_hbm, ordy_hbm,
    gin_hbm, gqkv_hbm, gout_hbm,
    gin_ref, gqkv_ref, gout_ref, out_sem,
    act, cot, wqkv, wout, ordx, ordy,
    send, recv, bsend, brecv,
    x_ref, c_ref, normed, proj, gm, gp, mixed, prob,
    nfx, nfy, mfx, cfull, gfull,
    grad, ring, summed, second, padded, zin, fin,
    plane_in, load_sem, a2a_s, a2a_r, fac_s, fac_r, ring_s, ring_r, sec_s, sec_r, z_s, z_r, fin_s, fin_r,
):
    band = lax.axis_index("band")
    batch = lax.axis_index("batch")
    y, zh, x = band // 16, (band // 4) % 4, band % 4
    zl, core = batch // 2, batch % 2
    z = zh * 2 + zl

    def at_x(d):
        return (y * 16 + zh * 4 + (x + d) % 4, batch)

    def at_y(d):
        return (((y + d) % 4) * 16 + zh * 4 + x, batch)

    def at_z(d):
        t = (z + d) % 8
        return (y * 16 + (t // 2) * 4 + x, (t % 2) * 2 + core)

    other = (band, zl * 2 + 1 - core)
    across = (band, (1 - zl) * 2 + core)
    corner = (band, (1 - zl) * 2 + 1 - core)

    loads = [
        pltpu.make_async_copy(src, dst, load_sem.at[i])
        for i, (src, dst) in enumerate(
            [(act_hbm, act), (cot_hbm, cot), (wqkv_hbm, wqkv), (ordx_hbm, ordx), (ordy_hbm, ordy), (wout_hbm, wout)]
        )
    ]
    loads[0].start()
    barrier = pltpu.get_barrier_semaphore()
    for k in range(1, 16):
        to = ((y + k // 4) % 4) * 16 + zh * 4 + (x + k % 4) % 4
        pl.semaphore_signal(barrier, 1, device_id=(to, batch), device_id_type=MESH)
    for d in range(1, 8):
        pl.semaphore_signal(barrier, 1, device_id=at_z(d), device_id_type=MESH)
    for to in (other, corner):
        pl.semaphore_signal(barrier, 1, device_id=to, device_id_type=MESH)
    for c in loads[1:]:
        c.start()

    fill = one_hot(128, 128, lambda o: ((o >> 2) & 1) * 64 + (o >> 3) * 4 + (o & 3))

    def pack(src, slot):
        for g in range(4):
            rows = pl.ds(g * 64, 64)
            stack = jnp.concatenate([src[rows, :384], src[rows, 384:]], axis=0)
            send[slot, pl.ds(g * 16, 16)] = dot(fill, stack).astype(BF).reshape(16, 8, 384)

    def push(group, src, dst, s, r):
        def one(dz, k):
            peer = ((y + k % 4) % 4) * 16 + ((zh + dz) % 4) * 4 + (x + k // 4) % 4
            pltpu.make_async_remote_copy(
                src_ref=src.at[peer],
                dst_ref=dst.at[band],
                send_sem=s.at[group],
                recv_sem=r.at[group],
                device_id=(peer, batch),
                device_id_type=MESH,
            ).start()

        def far(k, _):
            one(2, k)
            return 0

        def near(k, _):
            one(1, k)
            one(3, k)
            return 0

        def plane(k, _):
            one(0, k)
            return 0

        if group == 0:
            lax.fori_loop(0, 16, far, 0)
        elif group == 1:
            lax.fori_loop(0, 16, near, 0)
        else:
            lax.fori_loop(1, 16, plane, 0)
            dst[band] = src[band]

    def arrive(group, dst, sem):
        n = (16, 32, 15)[group]
        pltpu.make_async_copy(dst.at[pl.ds(0, n)], dst.at[pl.ds(0, n)], sem.at[group]).wait()

    pl.semaphore_wait(barrier, 24)
    for d in (2, 4, 6):
        pl.semaphore_signal(plane_in, 1, device_id=at_z(d), device_id_type=MESH)
    loads[0].wait()
    pack(act, 0)
    pl.semaphore_wait(plane_in, 3)
    for g in range(3):
        push(g, send.at[0], recv.at[0], a2a_s.at[0], a2a_r.at[0])
    loads[1].wait()
    pack(cot, 1)
    for g in range(3):
        push(g, send.at[1], recv.at[1], a2a_s.at[1], a2a_r.at[1])

    empty = one_hot(128, 128, lambda o: ((o & 15) << 3) + ((o >> 6) << 2) + ((o >> 4) & 3))

    def unpack(slot, dst):
        for blk in range(4):
            got = recv[slot, pl.ds(blk * 16, 16)].reshape(128, 384)
            out = dot(empty, got).astype(BF)
            for t in range(4):
                rows = pl.ds(t * 64 + blk * 16, 16)
                dst[rows, :384] = out[t * 16 : t * 16 + 16]
                dst[rows, 384:] = out[64 + t * 16 : 64 + t * 16 + 16]

    arrive(0, recv.at[0], a2a_r.at[0])
    arrive(2, recv.at[0], a2a_r.at[0])
    arrive(1, recv.at[0], a2a_r.at[0])
    unpack(0, x_ref)
    as_float = x_ref[...].astype(F32)
    inverse = lax.rsqrt(jnp.mean(as_float * as_float, axis=-1, keepdims=True) + EPSILON)
    normed[...] = (as_float * inverse).astype(BF)
    loads[2].wait()
    proj[...] = dot(normed[...], wqkv[...]).astype(BF)
    half = pl.ds(pl.multiple_of(core * 256, 256), 256)
    loads[3].wait()
    loads[4].wait()
    nfx[:, half] = dot(ordx[...], normed[...], 1, 1).astype(BF)
    nfy[:, half] = dot(ordy[...], normed[...], 1, 1).astype(BF)
    fx = remote(nfx.at[:, half], nfx.at[:, half], fac_s.at[0], fac_r.at[0], other)
    fy = remote(nfy.at[:, half], nfy.at[:, half], fac_s.at[1], fac_r.at[1], other)
    fx.start()
    fy.start()

    scale = HD ** (-0.5)
    lane = lax.broadcasted_iota(jnp.int32, (1, WIDE), 1) // HD
    masks = [lane == g for g in range(GROUP)]

    def spread(v):
        zero = jnp.zeros_like(v)
        return jnp.concatenate([jnp.where(m, v, zero) for m in masks], axis=0)

    def gather(r):
        out = r[0:64]
        for g in range(1, GROUP):
            out = jnp.where(masks[g], r[g * 64 : g * 64 + 64], out)
        return out

    each = [(c, h) for c in range(4) for h in range(PAIRS)]
    batches = [each[n : n + BATCH] for n in range(0, len(each), BATCH)]

    def take(ref, off, it):
        return [ref[pl.ds(c * 64, 64), off + h * WIDE : off + h * WIDE + WIDE] for c, h in it]

    def put(ref, it, values):
        for (c, h), v in zip(it, values):
            ref[pl.ds(c * 64, 64), h * WIDE : h * WIDE + WIDE] = v

    for it in batches:
        qs = [spread(t) for t in take(proj, 0, it)]
        s = [dot(k, q, 1, 1) * scale for k, q in zip(take(proj, 768, it), qs)]
        e = [jnp.exp(t - jnp.max(t, axis=0, keepdims=True)) for t in s]
        p = [t * (1.0 / jnp.sum(t, axis=0, keepdims=True)) for t in e]
        for (c, h), t in zip(it, p):
            prob[c * PAIRS + h] = t
        put(mixed, it, [gather(dot(t.astype(BF), v, 0, 0)).astype(BF) for t, v in zip(p, take(proj, 1536, it))])
    mfx[:, half] = dot(ordx[...], mixed[...], 1, 1).astype(BF)
    fm = remote(mfx.at[:, half], mfx.at[:, half], fac_s.at[2], fac_r.at[2], other)
    fm.start()

    own_c = pl.ds(pl.multiple_of(core * 384, 128), 384)
    their_c = pl.ds(pl.multiple_of((1 - core) * 384, 128), 384)
    loads[5].wait()
    for g in range(3):
        arrive(g, recv.at[1], a2a_r.at[1])
    unpack(1, c_ref)
    fc = remote(c_ref.at[:, their_c], cfull.at[half], fac_s.at[3], fac_r.at[3], other)
    fc.start()
    cfull[half] = c_ref[:, own_c]
    gm[...] = dot(c_ref[...], wout[...], 1, 1).astype(BF)
    for it in batches:
        gs = [spread(t) for t in take(gm, 0, it)]
        dp = [dot(v, g, 1, 1) for v, g in zip(take(proj, 1536, it), gs)]
        p = [prob[c * PAIRS + h] for c, h in it]
        put(gp.at[2], it, [dot(a.astype(BF), g).astype(BF) for a, g in zip(p, gs)])
        ds = [(a * (d - jnp.sum(a * d, axis=0, keepdims=True)) * scale).astype(BF) for a, d in zip(p, dp)]
        put(gp.at[0], it, [gather(dot(d, k, 0, 0)).astype(BF) for d, k in zip(ds, take(proj, 768, it))])
        qs = [spread(t) for t in take(proj, 0, it)]
        put(gp.at[1], it, [dot(d, q).astype(BF) for d, q in zip(ds, qs)])

    def share(s):
        cp = remote(gp.at[s, :, their_c], gfull.at[s, half], fac_s.at[4 + s], fac_r.at[4 + s], other)
        cp.start()
        gfull[s, half] = gp[s, :, own_c]
        return cp

    fv = share(2)
    fq = share(0)
    fk = share(1)

    def first_axis(m):
        return (x, at_x) if m % 2 == 0 else (y, at_y)

    def second_axis(m):
        return (y, at_y) if m % 2 == 0 else (x, at_x)

    def block(pos, part):
        return pl.ds(pl.multiple_of((pos % 4) * 192 + part * 96, 96), 96)

    def slot(m, i):
        return ring.at[m, i // 2, pl.ds((i % 2) * 96, 96)]

    def ring_copy(m, i, src, to):
        return remote(src, slot(m, i), ring_s.at[m, i], ring_r.at[m, i], to)

    def ring_start(m):
        pos, to = first_axis(m)
        g = grad.at[m]
        cps = [
            ring_copy(m, 0, g.at[block(pos + 2, 0)], to(1)),
            ring_copy(m, 1, g.at[block(pos + 2, 1)], to(3)),
            ring_copy(m, 2, g.at[block(pos + 3, 0)], to(3)),
            ring_copy(m, 3, g.at[block(pos + 1, 1)], to(1)),
        ]
        for c in cps[:2]:
            c.start()
        return cps

    def ring_near(cps):
        for c in cps[2:]:
            c.start()

    def ring_pass(m, cps):
        pos, to = first_axis(m)
        cps[0].wait_recv()
        b = block(pos + 1, 0)
        grad[m, b] = (grad[m, b].astype(F32) + slot(m, 0)[...].astype(F32)).astype(BF)
        cps.append(ring_copy(m, 4, grad.at[m, b], to(1)))
        cps[4].start()
        cps[1].wait_recv()
        b = block(pos + 3, 1)
        grad[m, b] = (grad[m, b].astype(F32) + slot(m, 1)[...].astype(F32)).astype(BF)
        cps.append(ring_copy(m, 5, grad.at[m, b], to(3)))
        cps[5].start()

    def ring_end(m, cps):
        pos, _ = first_axis(m)
        for c in cps[2:]:
            c.wait_recv()
        for part, i, j in ((0, 2, 4), (1, 3, 5)):
            t = grad[m, block(pos, part)].astype(F32) + slot(m, i)[...].astype(F32) + slot(m, j)[...].astype(F32)
            summed[m, pl.ds(part * 96, 96)] = t.astype(BF)

    def row48(pos):
        return pl.ds(pl.multiple_of((pos % 4) * 48, 48), 48)

    def second_start(m):
        pos, to = second_axis(m)
        cps = [
            remote(summed.at[m, row48(pos + d)], second.at[m, d - 1], sec_s.at[m, d - 1], sec_r.at[m, d - 1], to(d))
            for d in (2, 1, 3)
        ]
        for c in cps:
            c.start()
        return cps

    pad = one_hot(64, 48, lambda o: jnp.where((o & 15) < 12, (o >> 4) * 12 + (o & 15), -1))

    def second_end(m, cps):
        pos, _ = second_axis(m)
        for c in cps:
            c.wait_recv()
        t = summed[m, row48(pos)].astype(F32)
        for d in range(3):
            t = t + second[m, d].astype(F32)
        padded[m] = dot(pad, t.astype(BF)).astype(BF).reshape(4, 16, 384)

    def z_start(pair):
        out = []
        for d in (4, 3, 5, 2, 6, 1, 7):
            to = (z + d) % 8
            cp = remote(
                padded.at[pair * 2 + to % 2, to // 2], zin.at[pair, z], z_s.at[pair, d - 1], z_r.at[pair, d - 1], at_z(d)
            )
            cp.start()
            out.append(cp)
        zin[pair, z] = padded[pair * 2 + zl, zh]
        return out

    def z_end(pair, cps):
        for c in cps:
            c.wait_recv()
        t = zin[pair, 0].astype(F32)
        for i in range(1, 8):
            t = t + zin[pair, i].astype(F32)
        fin[pair, batch] = (t * (1.0 / 256.0)).astype(BF)
        out = []
        for i, to in enumerate((other, across, corner)):
            cp = remote(fin.at[pair, batch], fin.at[pair, batch], fin_s.at[pair, i], fin_r.at[pair, i], to)
            cp.start()
            out.append(cp)
        return out

    fm.wait_recv()
    fc.wait_recv()
    grad[0] = dot(mfx[...], cfull[...]).astype(BF)
    r0 = ring_start(0)
    fy.wait_recv()
    fv.wait_recv()
    grad[1] = dot(nfy[...], gfull[2]).astype(BF)
    r1 = ring_start(1)
    fx.wait_recv()
    fq.wait_recv()
    grad[2] = dot(nfx[...], gfull[0]).astype(BF)
    r2 = ring_start(2)
    fk.wait_recv()
    grad[3] = dot(nfy[...], gfull[1]).astype(BF)
    r3 = ring_start(3)
    ring_near(r0)
    ring_near(r1)
    ring_pass(0, r0)
    ring_pass(1, r1)
    ring_near(r2)
    ring_near(r3)
    gn = dot(gp[0], wqkv[:, :768], 1, 1) + dot(gp[1], wqkv[:, 768:1536], 1, 1) + dot(gp[2], wqkv[:, 1536:], 1, 1)
    xf = x_ref[...].astype(F32)
    centre = jnp.mean(gn * xf, axis=-1, keepdims=True)
    branch = (inverse * gn - xf * (inverse * inverse * inverse * centre)).astype(BF)
    back = one_hot(128, 128, lambda o: ((o >> 2) & 1) * 64 + (o & 3) * 16 + (o >> 3))
    for blk in range(4):
        stack = jnp.concatenate(
            [branch[t * 64 + blk * 16 : t * 64 + blk * 16 + 16, p * 384 : p * 384 + 384] for p in range(2) for t in range(4)],
            axis=0,
        )
        bsend[pl.ds(blk * 16, 16)] = dot(back, stack).astype(BF).reshape(16, 8, 384)
    ring_pass(2, r2)
    ring_pass(3, r3)
    for g in range(3):
        push(g, bsend, brecv, a2a_s.at[2], a2a_r.at[2])
    ring_end(0, r0)
    s0 = second_start(0)
    ring_end(1, r1)
    s1 = second_start(1)
    ring_end(2, r2)
    s2 = second_start(2)
    ring_end(3, r3)
    s3 = second_start(3)
    second_end(0, s0)
    second_end(1, s1)
    z0 = z_start(0)
    second_end(2, s2)
    second_end(3, s3)
    z1 = z_start(1)
    e0 = z_end(0, z0)
    for c in [fx, fy, fm, fc, fv, fq, fk] + r0 + r1 + r2 + r3 + s0 + s1 + s2 + s3:
        c.wait_send()
    for g in range(3):
        arrive(g, send.at[0], a2a_s.at[0])
        arrive(g, send.at[1], a2a_s.at[1])
    for g in range(3):
        arrive(g, brecv, a2a_r.at[2])
    home = one_hot(128, 128, lambda o: (((o & 63) >> 2) << 3) + ((o >> 6) << 2) + (o & 3))
    for blk in range(4):
        rows = pl.ds(blk * 64, 64)
        got = dot(home, brecv[pl.ds(blk * 16, 16)].reshape(128, 384))
        gin_ref[rows, :384] = (cot[rows, :384].astype(F32) + got[:64]).astype(BF)
        gin_ref[rows, 384:] = (cot[rows, 384:].astype(F32) + got[64:]).astype(BF)
    outs = [
        pltpu.make_async_copy(src, dst, out_sem.at[i])
        for i, (src, dst) in enumerate([(gin_ref, gin_hbm), (gqkv_ref, gqkv_hbm), (gout_ref, gout_hbm)])
    ]
    outs[0].start()
    e1 = z_end(1, z1)
    for g in range(3):
        arrive(g, bsend, a2a_s.at[2])
    for c in z0 + e0:
        c.wait_send()
    for pair, cps in ((0, e0), (1, e1)):
        for c in cps:
            c.wait_recv()
        for q in range(4):
            m = pair * 2 + q // 2
            at = (0, 1536, 0, 768)[m] + (q % 2) * 384
            dst = gout_ref if m == 0 else gqkv_ref
            dst[:, at : at + 384] = fin[pair, q].astype(F32)[:12]
        outs[2 - pair].start()
    for c in z1 + e1:
        c.wait_send()
    for c in outs:
        c.wait()


def hand_over(a, b, c, a_out, b_out, c_out, va, vb, vc, sem):
    here = [pltpu.make_async_copy(src, dst, sem.at[i]) for i, (src, dst) in enumerate([(a, va), (b, vb), (c, vc)])]
    away = [
        pltpu.make_async_copy(src, dst, sem.at[i + 3]) for i, (src, dst) in enumerate([(va, a_out), (vb, b_out), (vc, c_out)])
    ]
    for cp in here:
        cp.start()
    for first, then in zip(here, away):
        first.wait()
        then.start()
    for cp in away:
        cp.wait()


def orders():
    o = np.arange(768)
    a, b, c, i = o // 192, (o // 48) % 4, (o // 12) % 4, o % 12
    out = []
    for yy, xx in ((b, a), (a, b)):
        m = np.zeros((768, 768), np.float32)
        m[o, yy * 192 + c * 48 + xx * 12 + i] = 1.0
        out.append(jnp.asarray(m, dtype=BF))
    return out


def local(activations, cotangent, qkv_weight, out_weight):
    act = activations.reshape(256, 768)
    cot = cotangent.reshape(256, 768)
    ordx, ordy = orders()
    vm = pltpu.VMEM
    dma = pltpu.SemaphoreType.DMA
    hbm = pl.BlockSpec(memory_space=pltpu.HBM)
    gin, gqkv, gout = pl.pallas_call(
        body,
        out_shape=(
            jax.ShapeDtypeStruct((256, 768), BF),
            jax.ShapeDtypeStruct((12, 2304), F32),
            jax.ShapeDtypeStruct((12, 768), F32),
        ),
        in_specs=[hbm] * 6,
        out_specs=(hbm,) * 3,
        scratch_shapes=[
            vm((256, 768), BF),
            vm((12, 2304), F32),
            vm((12, 768), F32),
            dma((3,)),
            vm((256, 768), BF),
            vm((256, 768), BF),
            vm((768, 2304), BF),
            vm((768, 768), BF),
            vm((768, 768), BF),
            vm((768, 768), BF),
            vm((2, 64, 8, 384), BF),
            vm((2, 64, 8, 384), BF),
            vm((64, 8, 384), BF),
            vm((64, 8, 384), BF),
            vm((256, 768), BF),
            vm((256, 768), BF),
            vm((256, 768), BF),
            vm((256, 2304), BF),
            vm((256, 768), BF),
            vm((3, 256, 768), BF),
            vm((256, 768), BF),
            vm((4 * PAIRS, 64, WIDE), F32),
            vm((768, 512), BF),
            vm((768, 512), BF),
            vm((768, 512), BF),
            vm((512, 384), BF),
            vm((3, 512, 384), BF),
            vm((4, 768, 384), BF),
            vm((4, 3, 192, 384), BF),
            vm((4, 192, 384), BF),
            vm((4, 3, 48, 384), BF),
            vm((4, 4, 16, 384), BF),
            vm((2, 8, 16, 384), BF),
            vm((2, 4, 16, 384), BF),
            pltpu.SemaphoreType.REGULAR,
            dma((6,)),
            dma((3, 3)),
            dma((3, 3)),
            dma((7,)),
            dma((7,)),
            dma((4, 6)),
            dma((4, 6)),
            dma((4, 3)),
            dma((4, 3)),
            dma((2, 7)),
            dma((2, 7)),
            dma((2, 3)),
            dma((2, 3)),
        ],
        compiler_params=pltpu.CompilerParams(collective_id=0, has_side_effects=True, vmem_limit_bytes=62 << 20),
        name="column_backward",
    )(act, cot, qkv_weight, out_weight, ordx, ordy)
    gin, gqkv, gout = pl.pallas_call(
        hand_over,
        out_shape=tuple(jax.ShapeDtypeStruct(v.shape, v.dtype) for v in (gin, gqkv, gout)),
        in_specs=[hbm] * 3,
        out_specs=(hbm,) * 3,
        scratch_shapes=[vm((256, 768), BF), vm((12, 2304), F32), vm((12, 768), F32), dma((6,))],
        name="hand_over",
    )(gin, gqkv, gout)
    return gin.reshape(activations.shape), gqkv, gout


def solution(mesh):
    return jax.shard_map(
        local,
        mesh=mesh,
        in_specs=(P("batch", "band", None, None), P("batch", "band", None, None), P(), P()),
        out_specs=(P("batch", "band", None, None), P("band", None), P("band", None)),
        check_vma=False,
    )
```

```python
import functools

import jax
import jax.numpy as jnp
import numpy as np
from jax import lax
from jax.experimental import pallas as pl
from jax.experimental.pallas import tpu as pltpu
from jax.sharding import PartitionSpec as P

HEADS = 12
HD = 64
EPSILON = 1e-06
MESH = pl.DeviceIdType.MESH
BF = jnp.bfloat16
F32 = jnp.float32
GROUP = 4
WIDE = GROUP * HD
PAIRS = HEADS // GROUP
BATCH = 6


def one_hot(rows, cols, index):
    o = lax.broadcasted_iota(jnp.int32, (rows, cols), 0)
    i = lax.broadcasted_iota(jnp.int32, (rows, cols), 1)
    return jnp.where(index(o) == i, 1.0, 0.0).astype(BF)


def dot(a, b, ca=1, cb=0):
    return lax.dot_general(a, b, (((ca,), (cb,)), ((), ())), preferred_element_type=F32)


def remote(src, dst, s, r, to):
    return pltpu.make_async_remote_copy(
        src_ref=src, dst_ref=dst, send_sem=s, recv_sem=r, device_id=to, device_id_type=MESH
    )


def body(
    act_hbm, cot_hbm, wqkv_hbm, wout_hbm, ordx_hbm, ordy_hbm,
    gin_hbm, gqkv_hbm, gout_hbm,
    gin_ref, gqkv_ref, gout_ref, out_sem,
    act, cot, wqkv, wout, ordx, ordy,
    send, recv, bsend, brecv,
    x_ref, c_ref, normed, proj, gm, gp, mixed, prob,
    nfx, nfy, mfx, cfull, gfull,
    grad, ring, summed, second, padded, zin, fin,
    plane_in, load_sem, a2a_s, a2a_r, fac_s, fac_r, ring_s, ring_r, sec_s, sec_r, z_s, z_r, fin_s, fin_r,
):
    band = lax.axis_index("band")
    batch = lax.axis_index("batch")
    y, zh, x = band // 16, (band // 4) % 4, band % 4
    zl, core = batch // 2, batch % 2
    z = zh * 2 + zl

    def at_x(d):
        return (y * 16 + zh * 4 + (x + d) % 4, batch)

    def at_y(d):
        return (((y + d) % 4) * 16 + zh * 4 + x, batch)

    def at_z(d):
        t = (z + d) % 8
        return (y * 16 + (t // 2) * 4 + x, (t % 2) * 2 + core)

    other = (band, zl * 2 + 1 - core)
    across = (band, (1 - zl) * 2 + core)
    corner = (band, (1 - zl) * 2 + 1 - core)

    loads = [
        pltpu.make_async_copy(src, dst, load_sem.at[i])
        for i, (src, dst) in enumerate(
            [(act_hbm, act), (cot_hbm, cot), (wqkv_hbm, wqkv), (ordx_hbm, ordx), (ordy_hbm, ordy), (wout_hbm, wout)]
        )
    ]
    loads[0].start()
    barrier = pltpu.get_barrier_semaphore()
    for k in range(1, 16):
        to = ((y + k // 4) % 4) * 16 + zh * 4 + (x + k % 4) % 4
        pl.semaphore_signal(barrier, 1, device_id=(to, batch), device_id_type=MESH)
    for d in range(1, 8):
        pl.semaphore_signal(barrier, 1, device_id=at_z(d), device_id_type=MESH)
    for to in (other, corner):
        pl.semaphore_signal(barrier, 1, device_id=to, device_id_type=MESH)
    for c in loads[1:]:
        c.start()

    fill = one_hot(128, 128, lambda o: ((o >> 2) & 1) * 64 + (o >> 3) * 4 + (o & 3))

    def pack(src, slot):
        for g in range(4):
            rows = pl.ds(g * 64, 64)
            stack = jnp.concatenate([src[rows, :384], src[rows, 384:]], axis=0)
            send[slot, pl.ds(g * 16, 16)] = dot(fill, stack).astype(BF).reshape(16, 8, 384)

    def push(group, src, dst, s, r):
        def one(dz, k):
            peer = ((y + k % 4) % 4) * 16 + ((zh + dz) % 4) * 4 + (x + k // 4) % 4
            pltpu.make_async_remote_copy(
                src_ref=src.at[peer],
                dst_ref=dst.at[band],
                send_sem=s.at[group],
                recv_sem=r.at[group],
                device_id=(peer, batch),
                device_id_type=MESH,
            ).start()

        def far(k, _):
            one(2, k)
            return 0

        def near(k, _):
            one(1, k)
            one(3, k)
            return 0

        def plane(k, _):
            one(0, k)
            return 0

        if group == 0:
            lax.fori_loop(0, 16, far, 0)
        elif group == 1:
            lax.fori_loop(0, 16, near, 0)
        else:
            lax.fori_loop(1, 16, plane, 0)
            dst[band] = src[band]

    def arrive(group, dst, sem):
        n = (16, 32, 15)[group]
        pltpu.make_async_copy(dst.at[pl.ds(0, n)], dst.at[pl.ds(0, n)], sem.at[group]).wait()

    pl.semaphore_wait(barrier, 24)
    for d in (2, 4, 6):
        pl.semaphore_signal(plane_in, 1, device_id=at_z(d), device_id_type=MESH)
    loads[0].wait()
    pack(act, 0)
    pl.semaphore_wait(plane_in, 3)
    for g in range(3):
        push(g, send.at[0], recv.at[0], a2a_s.at[0], a2a_r.at[0])
    loads[1].wait()
    pack(cot, 1)
    for g in range(3):
        push(g, send.at[1], recv.at[1], a2a_s.at[1], a2a_r.at[1])

    empty = one_hot(128, 128, lambda o: ((o & 15) << 3) + ((o >> 6) << 2) + ((o >> 4) & 3))

    def unpack(slot, dst):
        for blk in range(4):
            got = recv[slot, pl.ds(blk * 16, 16)].reshape(128, 384)
            out = dot(empty, got).astype(BF)
            for t in range(4):
                rows = pl.ds(t * 64 + blk * 16, 16)
                dst[rows, :384] = out[t * 16 : t * 16 + 16]
                dst[rows, 384:] = out[64 + t * 16 : 64 + t * 16 + 16]

    arrive(0, recv.at[0], a2a_r.at[0])
    arrive(2, recv.at[0], a2a_r.at[0])
    arrive(1, recv.at[0], a2a_r.at[0])
    unpack(0, x_ref)
    as_float = x_ref[...].astype(F32)
    inverse = lax.rsqrt(jnp.mean(as_float * as_float, axis=-1, keepdims=True) + EPSILON)
    normed[...] = (as_float * inverse).astype(BF)
    loads[2].wait()
    proj[...] = dot(normed[...], wqkv[...]).astype(BF)
    half = pl.ds(pl.multiple_of(core * 256, 256), 256)
    loads[3].wait()
    loads[4].wait()
    nfx[:, half] = dot(ordx[...], normed[...], 1, 1).astype(BF)
    nfy[:, half] = dot(ordy[...], normed[...], 1, 1).astype(BF)
    fx = remote(nfx.at[:, half], nfx.at[:, half], fac_s.at[0], fac_r.at[0], other)
    fy = remote(nfy.at[:, half], nfy.at[:, half], fac_s.at[1], fac_r.at[1], other)
    fx.start()
    fy.start()

    scale = HD ** (-0.5)
    lane = lax.broadcasted_iota(jnp.int32, (1, WIDE), 1) // HD
    masks = [lane == g for g in range(GROUP)]

    def spread(v):
        zero = jnp.zeros_like(v)
        return jnp.concatenate([jnp.where(m, v, zero) for m in masks], axis=0)

    def gather(r):
        out = r[0:64]
        for g in range(1, GROUP):
            out = jnp.where(masks[g], r[g * 64 : g * 64 + 64], out)
        return out

    each = [(c, h) for c in range(4) for h in range(PAIRS)]
    batches = [each[n : n + BATCH] for n in range(0, len(each), BATCH)]

    def take(ref, off, it):
        return [ref[pl.ds(c * 64, 64), off + h * WIDE : off + h * WIDE + WIDE] for c, h in it]

    def put(ref, it, values):
        for (c, h), v in zip(it, values):
            ref[pl.ds(c * 64, 64), h * WIDE : h * WIDE + WIDE] = v

    for it in batches:
        qs = [spread(t) for t in take(proj, 0, it)]
        s = [dot(k, q, 1, 1) * scale for k, q in zip(take(proj, 768, it), qs)]
        e = [jnp.exp(t - jnp.max(t, axis=0, keepdims=True)) for t in s]
        p = [t * (1.0 / jnp.sum(t, axis=0, keepdims=True)) for t in e]
        for (c, h), t in zip(it, p):
            prob[c * PAIRS + h] = t
        put(mixed, it, [gather(dot(t.astype(BF), v, 0, 0)).astype(BF) for t, v in zip(p, take(proj, 1536, it))])
    mfx[:, half] = dot(ordx[...], mixed[...], 1, 1).astype(BF)
    fm = remote(mfx.at[:, half], mfx.at[:, half], fac_s.at[2], fac_r.at[2], other)
    fm.start()

    own_c = pl.ds(pl.multiple_of(core * 384, 128), 384)
    their_c = pl.ds(pl.multiple_of((1 - core) * 384, 128), 384)
    loads[5].wait()
    for g in range(3):
        arrive(g, recv.at[1], a2a_r.at[1])
    unpack(1, c_ref)
    fc = remote(c_ref.at[:, their_c], cfull.at[half], fac_s.at[3], fac_r.at[3], other)
    fc.start()
    cfull[half] = c_ref[:, own_c]
    gm[...] = dot(c_ref[...], wout[...], 1, 1).astype(BF)
    def share(n):
        out = []
        for s in (2, 0, 1):
            rows = pl.ds(n * 128, 128)
            into = pl.ds(pl.multiple_of(core * 256 + n * 128, 128), 128)
            cp = remote(
                gp.at[s, rows, their_c], gfull.at[s, into], fac_s.at[4 + s * 2 + n], fac_r.at[4 + s * 2 + n], other
            )
            cp.start()
            gfull[s, into] = gp[s, rows, own_c]
            out.append(cp)
        return out

    shared = []
    for n, it in enumerate(batches):
        gs = [spread(t) for t in take(gm, 0, it)]
        dp = [dot(v, g, 1, 1) for v, g in zip(take(proj, 1536, it), gs)]
        p = [prob[c * PAIRS + h] for c, h in it]
        put(gp.at[2], it, [dot(a.astype(BF), g).astype(BF) for a, g in zip(p, gs)])
        ds = [(a * (d - jnp.sum(a * d, axis=0, keepdims=True)) * scale).astype(BF) for a, d in zip(p, dp)]
        put(gp.at[0], it, [gather(dot(d, k, 0, 0)).astype(BF) for d, k in zip(ds, take(proj, 768, it))])
        qs = [spread(t) for t in take(proj, 0, it)]
        put(gp.at[1], it, [dot(d, q).astype(BF) for d, q in zip(ds, qs)])
        shared.append(share(n))
    fv, fq, fk = [[a, b] for a, b in zip(*shared)]

    def first_axis(m):
        return (x, at_x) if m % 2 == 0 else (y, at_y)

    def second_axis(m):
        return (y, at_y) if m % 2 == 0 else (x, at_x)

    def block(pos, part):
        return pl.ds(pl.multiple_of((pos % 4) * 192 + part * 96, 96), 96)

    def slot(m, i):
        return ring.at[m, i // 2, pl.ds((i % 2) * 96, 96)]

    def ring_copy(m, i, src, to):
        return remote(src, slot(m, i), ring_s.at[m, i], ring_r.at[m, i], to)

    def ring_start(m):
        pos, to = first_axis(m)
        g = grad.at[m]
        cps = [
            ring_copy(m, 0, g.at[block(pos + 2, 0)], to(1)),
            ring_copy(m, 1, g.at[block(pos + 2, 1)], to(3)),
            ring_copy(m, 2, g.at[block(pos + 3, 0)], to(3)),
            ring_copy(m, 3, g.at[block(pos + 1, 1)], to(1)),
        ]
        for c in cps[:2]:
            c.start()
        return cps

    def ring_near(cps):
        for c in cps[2:]:
            c.start()

    def ring_pass(m, cps):
        pos, to = first_axis(m)
        cps[0].wait_recv()
        b = block(pos + 1, 0)
        grad[m, b] = (grad[m, b].astype(F32) + slot(m, 0)[...].astype(F32)).astype(BF)
        cps.append(ring_copy(m, 4, grad.at[m, b], to(1)))
        cps[4].start()
        cps[1].wait_recv()
        b = block(pos + 3, 1)
        grad[m, b] = (grad[m, b].astype(F32) + slot(m, 1)[...].astype(F32)).astype(BF)
        cps.append(ring_copy(m, 5, grad.at[m, b], to(3)))
        cps[5].start()

    def ring_end(m, cps):
        pos, _ = first_axis(m)
        for c in cps[2:]:
            c.wait_recv()
        for part, i, j in ((0, 2, 4), (1, 3, 5)):
            t = grad[m, block(pos, part)].astype(F32) + slot(m, i)[...].astype(F32) + slot(m, j)[...].astype(F32)
            summed[m, pl.ds(part * 96, 96)] = t.astype(BF)

    def row48(pos):
        return pl.ds(pl.multiple_of((pos % 4) * 48, 48), 48)

    def second_start(m):
        pos, to = second_axis(m)
        cps = [
            remote(summed.at[m, row48(pos + d)], second.at[m, d - 1], sec_s.at[m, d - 1], sec_r.at[m, d - 1], to(d))
            for d in (2, 1, 3)
        ]
        for c in cps:
            c.start()
        return cps

    pad = one_hot(64, 48, lambda o: jnp.where((o & 15) < 12, (o >> 4) * 12 + (o & 15), -1))

    def second_end(m, cps):
        pos, _ = second_axis(m)
        for c in cps:
            c.wait_recv()
        t = summed[m, row48(pos)].astype(F32)
        for d in range(3):
            t = t + second[m, d].astype(F32)
        padded[m] = dot(pad, t.astype(BF)).astype(BF).reshape(4, 16, 384)

    def z_start(pair):
        out = []
        for d in (4, 3, 5, 2, 6, 1, 7):
            to = (z + d) % 8
            cp = remote(
                padded.at[pair * 2 + to % 2, to // 2], zin.at[pair, z], z_s.at[pair, d - 1], z_r.at[pair, d - 1], at_z(d)
            )
            cp.start()
            out.append(cp)
        zin[pair, z] = padded[pair * 2 + zl, zh]
        return out

    def z_end(pair, cps):
        for c in cps:
            c.wait_recv()
        t = zin[pair, 0].astype(F32)
        for i in range(1, 8):
            t = t + zin[pair, i].astype(F32)
        fin[pair, batch] = (t * (1.0 / 256.0)).astype(BF)
        out = []
        for i, to in enumerate((other, across, corner)):
            cp = remote(fin.at[pair, batch], fin.at[pair, batch], fin_s.at[pair, i], fin_r.at[pair, i], to)
            cp.start()
            out.append(cp)
        return out

    fm.wait_recv()
    fc.wait_recv()
    grad[0] = dot(mfx[...], cfull[...]).astype(BF)
    r0 = ring_start(0)
    fy.wait_recv()
    for c in fv:
        c.wait_recv()
    grad[1] = dot(nfy[...], gfull[2]).astype(BF)
    r1 = ring_start(1)
    fx.wait_recv()
    for c in fq:
        c.wait_recv()
    grad[2] = dot(nfx[...], gfull[0]).astype(BF)
    r2 = ring_start(2)
    for c in fk:
        c.wait_recv()
    grad[3] = dot(nfy[...], gfull[1]).astype(BF)
    r3 = ring_start(3)
    ring_near(r0)
    ring_near(r1)
    ring_pass(0, r0)
    ring_pass(1, r1)
    ring_near(r2)
    ring_near(r3)
    gn = dot(gp[0], wqkv[:, :768], 1, 1) + dot(gp[1], wqkv[:, 768:1536], 1, 1) + dot(gp[2], wqkv[:, 1536:], 1, 1)
    xf = x_ref[...].astype(F32)
    centre = jnp.mean(gn * xf, axis=-1, keepdims=True)
    branch = (inverse * gn - xf * (inverse * inverse * inverse * centre)).astype(BF)
    back = one_hot(128, 128, lambda o: ((o >> 2) & 1) * 64 + (o & 3) * 16 + (o >> 3))
    for blk in range(4):
        stack = jnp.concatenate(
            [branch[t * 64 + blk * 16 : t * 64 + blk * 16 + 16, p * 384 : p * 384 + 384] for p in range(2) for t in range(4)],
            axis=0,
        )
        bsend[pl.ds(blk * 16, 16)] = dot(back, stack).astype(BF).reshape(16, 8, 384)
    ring_pass(2, r2)
    ring_pass(3, r3)
    for g in range(3):
        push(g, bsend, brecv, a2a_s.at[2], a2a_r.at[2])
    ring_end(0, r0)
    s0 = second_start(0)
    ring_end(1, r1)
    s1 = second_start(1)
    ring_end(2, r2)
    s2 = second_start(2)
    ring_end(3, r3)
    s3 = second_start(3)
    second_end(0, s0)
    second_end(1, s1)
    z0 = z_start(0)
    second_end(2, s2)
    second_end(3, s3)
    z1 = z_start(1)
    e0 = z_end(0, z0)
    for c in [fx, fy, fm, fc] + fv + fq + fk + r0 + r1 + r2 + r3 + s0 + s1 + s2 + s3:
        c.wait_send()
    for g in range(3):
        arrive(g, send.at[0], a2a_s.at[0])
        arrive(g, send.at[1], a2a_s.at[1])
    for g in range(3):
        arrive(g, brecv, a2a_r.at[2])
    home = one_hot(128, 128, lambda o: (((o & 63) >> 2) << 3) + ((o >> 6) << 2) + (o & 3))
    for blk in range(4):
        rows = pl.ds(blk * 64, 64)
        got = dot(home, brecv[pl.ds(blk * 16, 16)].reshape(128, 384))
        gin_ref[rows, :384] = (cot[rows, :384].astype(F32) + got[:64]).astype(BF)
        gin_ref[rows, 384:] = (cot[rows, 384:].astype(F32) + got[64:]).astype(BF)
    outs = [
        pltpu.make_async_copy(src, dst, out_sem.at[i])
        for i, (src, dst) in enumerate([(gin_ref, gin_hbm), (gqkv_ref, gqkv_hbm), (gout_ref, gout_hbm)])
    ]
    outs[0].start()
    e1 = z_end(1, z1)
    for g in range(3):
        arrive(g, bsend, a2a_s.at[2])
    for c in z0 + e0:
        c.wait_send()
    for pair, cps in ((0, e0), (1, e1)):
        for c in cps:
            c.wait_recv()
        for q in range(4):
            m = pair * 2 + q // 2
            at = (0, 1536, 0, 768)[m] + (q % 2) * 384
            dst = gout_ref if m == 0 else gqkv_ref
            dst[:, at : at + 384] = fin[pair, q].astype(F32)[:12]
        outs[2 - pair].start()
    for c in z1 + e1:
        c.wait_send()
    for c in outs:
        c.wait()


def hand_over(a, b, c, a_out, b_out, c_out, va, vb, vc, sem):
    here = [pltpu.make_async_copy(src, dst, sem.at[i]) for i, (src, dst) in enumerate([(a, va), (b, vb), (c, vc)])]
    away = [
        pltpu.make_async_copy(src, dst, sem.at[i + 3]) for i, (src, dst) in enumerate([(va, a_out), (vb, b_out), (vc, c_out)])
    ]
    for cp in here:
        cp.start()
    for first, then in zip(here, away):
        first.wait()
        then.start()
    for cp in away:
        cp.wait()


def orders():
    o = np.arange(768)
    a, b, c, i = o // 192, (o // 48) % 4, (o // 12) % 4, o % 12
    out = []
    for yy, xx in ((b, a), (a, b)):
        m = np.zeros((768, 768), np.float32)
        m[o, yy * 192 + c * 48 + xx * 12 + i] = 1.0
        out.append(jnp.asarray(m, dtype=BF))
    return out


def local(activations, cotangent, qkv_weight, out_weight):
    act = activations.reshape(256, 768)
    cot = cotangent.reshape(256, 768)
    ordx, ordy = orders()
    vm = pltpu.VMEM
    dma = pltpu.SemaphoreType.DMA
    hbm = pl.BlockSpec(memory_space=pltpu.HBM)
    gin, gqkv, gout = pl.pallas_call(
        body,
        out_shape=(
            jax.ShapeDtypeStruct((256, 768), BF),
            jax.ShapeDtypeStruct((12, 2304), F32),
            jax.ShapeDtypeStruct((12, 768), F32),
        ),
        in_specs=[hbm] * 6,
        out_specs=(hbm,) * 3,
        scratch_shapes=[
            vm((256, 768), BF),
            vm((12, 2304), F32),
            vm((12, 768), F32),
            dma((3,)),
            vm((256, 768), BF),
            vm((256, 768), BF),
            vm((768, 2304), BF),
            vm((768, 768), BF),
            vm((768, 768), BF),
            vm((768, 768), BF),
            vm((2, 64, 8, 384), BF),
            vm((2, 64, 8, 384), BF),
            vm((64, 8, 384), BF),
            vm((64, 8, 384), BF),
            vm((256, 768), BF),
            vm((256, 768), BF),
            vm((256, 768), BF),
            vm((256, 2304), BF),
            vm((256, 768), BF),
            vm((3, 256, 768), BF),
            vm((256, 768), BF),
            vm((4 * PAIRS, 64, WIDE), F32),
            vm((768, 512), BF),
            vm((768, 512), BF),
            vm((768, 512), BF),
            vm((512, 384), BF),
            vm((3, 512, 384), BF),
            vm((4, 768, 384), BF),
            vm((4, 3, 192, 384), BF),
            vm((4, 192, 384), BF),
            vm((4, 3, 48, 384), BF),
            vm((4, 4, 16, 384), BF),
            vm((2, 8, 16, 384), BF),
            vm((2, 4, 16, 384), BF),
            pltpu.SemaphoreType.REGULAR,
            dma((6,)),
            dma((3, 3)),
            dma((3, 3)),
            dma((10,)),
            dma((10,)),
            dma((4, 6)),
            dma((4, 6)),
            dma((4, 3)),
            dma((4, 3)),
            dma((2, 7)),
            dma((2, 7)),
            dma((2, 3)),
            dma((2, 3)),
        ],
        compiler_params=pltpu.CompilerParams(collective_id=0, has_side_effects=True, vmem_limit_bytes=62 << 20),
        name="column_backward",
    )(act, cot, qkv_weight, out_weight, ordx, ordy)
    gin, gqkv, gout = pl.pallas_call(
        hand_over,
        out_shape=tuple(jax.ShapeDtypeStruct(v.shape, v.dtype) for v in (gin, gqkv, gout)),
        in_specs=[hbm] * 3,
        out_specs=(hbm,) * 3,
        scratch_shapes=[vm((256, 768), BF), vm((12, 2304), F32), vm((12, 768), F32), dma((6,))],
        name="hand_over",
    )(gin, gqkv, gout)
    return gin.reshape(activations.shape), gqkv, gout


def solution(mesh):
    return jax.shard_map(
        local,
        mesh=mesh,
        in_specs=(P("batch", "band", None, None), P("batch", "band", None, None), P(), P()),
        out_specs=(P("batch", "band", None, None), P("band", None), P("band", None)),
        check_vma=False,
    )
```
